256 devices in a mesh: ia: 8 (over x, z_lo), ja: 8 (over z_hi, core), ka: 4 (over y).
Axes of the slice: x: 4, y: 4, z: 8 (z_hi: 4, z_lo: 2; z = z_hi * 2 + z_lo), core: 2. Of those that a mesh axis runs over, the one named last changes fastest.
Arguments:
- tokens: bfloat16 [8, 384, 8192], P('ja', 'ia', 'ka'), may hold values from -6 to 6
- weight_up: bfloat16 [8192, 24576], P('ka', ('ia', 'ja')), may hold values from -0.1875 to 0.1875
- cotangent: bfloat16 [8, 384, 24576], P('ja', None, ('ia', 'ka')), may hold values from -6 to 6
Outputs:
- active: bfloat16 [8, 384, 24576], P('ja', None, ('ia', 'ka'))
- weight_grad: float32 [8192, 24576], P('ka', ('ia', 'ja'))
The draws below stay inside these ranges and needn't reach their ends.
All inputs are finite; a program needn't handle non-finite values.
Results may differ from the reference program's by a relative error of at most 0.02.
Values may be sent and summed in bfloat16 or wider, within the bound.
A program may use at most 128 MiB of HBM per device.

```python
import jax
import jax.numpy as jnp
from jax import lax

D = 8192
FF = 24576
GROUP_TOK = 384
TOKENS = 3072
N_JA = 8


def spiked(drawn, rng, source, target, shards_of, factor):
    def block_of(dim):
        return (jnp.arange(drawn.shape[dim]) // (drawn.shape[dim] // shards_of)).reshape((-1,) + (1,) * (drawn.ndim - 1 - dim))

    near = jax.random.permutation(rng, shards_of)[block_of(target)]
    far = (block_of(target) + shards_of // 2) % shards_of
    return jnp.where((block_of(source) == near) | (block_of(source) == far), factor * drawn, drawn)


def levels(rng, extent, pieces, least, largest):
    gain = 1.0
    for axis_at, blocks in pieces:
        draws = jax.random.uniform(jax.random.fold_in(jax.random.fold_in(rng, 6), axis_at), (blocks,), jnp.float32, least / len(pieces), largest / len(pieces))
        gain = gain * jnp.repeat(jnp.exp(draws), extent[axis_at] // blocks).reshape((-1,) + (1,) * (len(extent) - 1 - axis_at))
    return gain


def gaussian(key, extent, deviation, limit, split=(), kind=jnp.bfloat16):
    loudness = levels(key, extent, split, -0.22, 0.18) if split else 1.0
    result = jax.random.normal(key, extent, jnp.float32) * deviation * loudness
    return jnp.minimum(jnp.maximum(result, -limit), limit).astype(kind)


def noise_with(rng, shape, deviation, reach, pieces, heavy, kind=jnp.bfloat16):
    drawn = deviation * jax.random.normal(rng, shape, jnp.float32)
    if pieces:
        drawn = drawn * levels(rng, shape, pieces, -0.22, 0.18)
    return jnp.clip(spiked(drawn, jax.random.fold_in(rng, 3), *heavy), -reach, reach).astype(kind)


def setup_inputs(seed: int = 0) -> dict:
    arg_keys = jax.random.split(jax.random.key(seed), 4)
    tokens = gaussian(arg_keys[0], (N_JA, GROUP_TOK, D), 1.0, 6.0, ((0, 8), (1, 8), (2, 4)))
    weight_up = noise_with(arg_keys[1], (D, FF), D ** -0.5, 0.1875, ((0, 4), (1, 64)), (0, 1, 64, 4.0))
    cotangent = noise_with(arg_keys[2], (N_JA, GROUP_TOK, FF), 1.0, 6.0, ((0, 8), (2, 32)), (0, 2, 8, 2.0))
    return {"tokens": tokens, "weight_up": weight_up, "cotangent": cotangent}


def gelu_tanh(value):
    return jax.nn.gelu(value, approximate=True)

def gelu_slope(pre, cotan):
    _, backward = jax.vjp(gelu_tanh, pre)
    return backward(cotan)[0]

def reference(tokens, weight_up, cotangent):
    flat_rows = tokens.reshape(TOKENS, D)
    pre = jnp.dot(flat_rows, weight_up, preferred_element_type=jnp.float32)
    active = gelu_tanh(pre).astype(jnp.bfloat16).reshape(N_JA, GROUP_TOK, FF)
    slope = gelu_slope(pre, cotangent.reshape(TOKENS, FF).astype(jnp.float32)).astype(jnp.bfloat16)
    slope_groups = slope.reshape(N_JA, GROUP_TOK, FF)

    def add_group(total, members):
        group_rows, group_slope = members
        partial_sum = lax.dot_general(group_rows, group_slope, (((0,), (0,)), ((), ())), preferred_element_type=jnp.float32)
        rounded = lax.optimization_barrier(partial_sum.astype(jnp.bfloat16)).astype(jnp.float32)
        return (total + rounded, None)
    weight_grad, _ = lax.scan(add_group, jnp.zeros((D, FF), jnp.float32), (tokens, slope_groups))
    return (active, weight_grad)
```

```python
import jax
import jax.numpy as jnp
from jax import lax
from jax.experimental import pallas as pl
from jax.experimental.pallas import tpu as pltpu
from jax.sharding import PartitionSpec as P

MESH = pl.DeviceIdType.MESH
ROWS, DEPTH, COLS = 48, 2048, 384
HALF = DEPTH // 2
PAIRS = ((1, 7), (0, 2), (3, 5), (6, 4))
ORDER = (
    (0, 0), (0, 1), (0, 2), (0, 3),
    (1, 0), (3, 0), (1, 1), (3, 1), (2, 0), (1, 2), (3, 2), (2, 1),
    (1, 3), (3, 3), (2, 2), (2, 3),
)
CHUNKS = len(ORDER)
SLOT = {(dx, dz): (n, i) for n, (dx, p) in enumerate(ORDER) for i, dz in enumerate(PAIRS[p])}
OFF_X = tuple(dx for dx, _ in ORDER)
OFF_Z = tuple(PAIRS[p] for _, p in ORDER)
GRAD_LAG = 3


def pick(index, table):
    out = jnp.int32(table[0])
    for j, entry in enumerate(table[1:], 1):
        out = jnp.where(index == j, jnp.int32(entry), out)
    return out


def mod(value, n):
    return lax.rem(value + 16 * n, n)


def kernel(tok_ref, w_ref, cot_ref, act_ref, grad_ref, xs, ws, cots, hop, mine, pf, pb, terms, slopes, acts,
           load_sem, z_send, z_recv, x_send, x_recv, sib_send, sib_recv, rs_send, rs_recv, ag_send, ag_recv,
           hop_send, hop_recv, mine_send, mine_recv, act_send, act_recv):
    ia, ja, y = lax.axis_index("ia"), lax.axis_index("ja"), lax.axis_index("ka")
    x, z_lo, z_hi, c = ia // 2, lax.rem(ia, 2), ja // 2, lax.rem(ja, 2)
    z = z_hi * 2 + z_lo

    def device(dx=0, dz=0, dy=0):
        tz = mod(z + dz, 8)
        return (mod(x + dx, 4) * 2 + lax.rem(tz, 2), (tz // 2) * 2 + c, mod(y + dy, 4))

    sibling = (ia, z_hi * 2 + 1 - c, y)

    def remote(src, dst, send, recv, to):
        return pltpu.make_async_remote_copy(
            src_ref=src, dst_ref=dst, send_sem=send, recv_sem=recv, device_id=to, device_id_type=MESH)

    loads = [
        pltpu.make_async_copy(tok_ref, xs.at[SLOT[0, 0][0], SLOT[0, 0][1], 0], load_sem.at[0]),
        pltpu.make_async_copy(cot_ref, cots, load_sem.at[1]),
        pltpu.make_async_copy(w_ref, ws, load_sem.at[2]),
    ]
    for load in loads:
        load.start()

    barrier = pltpu.get_barrier_semaphore()
    for to in [device(dx=1), device(dx=-1), device(dz=1), device(dz=-1)] + [device(dy=r) for r in (1, 2, 3)] + [
            (ia, mod(ja + d, 8), y) for d in range(1, 8)]:
        pl.semaphore_signal(barrier, inc=1, device_id=to, device_id_type=MESH)
    at_home = y == z_hi
    for owner in range(4):
        for core in range(2):
            @pl.when(jnp.logical_not(at_home & (owner == y) & (core == c)))
            def _():
                pl.semaphore_signal(barrier, inc=1, device_id=(ia, y * 2 + core, owner), device_id_type=MESH)
    pl.semaphore_wait(barrier, 14 + 8 - jnp.where(at_home, 1, 0))

    def block(dx, dz, core=0):
        n, i = SLOT[dx, dz]
        return xs.at[n, i, core]

    def half(ref, h):
        return ref.at[:, pl.ds(h * HALF, HALF)]

    def z_copy(dz, way, dst_dz):
        src = block(0, dz)
        if dst_dz == 4:
            h = 0 if way == 1 else 1
            return remote(half(src, h), half(block(0, 4), h), z_send.at[h * 4], z_recv.at[h * 4], device(dz=way))
        return remote(src, block(0, dst_dz), z_send.at[dst_dz], z_recv.at[dst_dz], device(dz=way))

    def x_copy(dz, way):
        dx = way % 4
        return remote(block(0, dz), block(dx, dz), x_send.at[dx, dz], x_recv.at[dx, dz], device(dx=way))

    def x_half(dz, way):
        h = 0 if way == 1 else 1
        return remote(half(block(way % 4, dz), h), half(block(2, dz), h), x_send.at[h * 2, dz], x_recv.at[h * 2, dz],
                      device(dx=way))

    def sib_copy(n, i):
        return remote(xs.at[n, i, 0], xs.at[n, i, 1], sib_send.at[n, i], sib_recv.at[n, i], sibling)

    def to_sibling(dx, dz):
        sib_copy(*SLOT[dx, dz]).start()

    def z_arrive(step):
        if step == 4:
            z_copy(3, 1, 4).wait_recv()
            z_copy(5, -1, 4).wait_recv()
            to_sibling(0, 4)
            return
        z_copy(step - 1, 1, step).wait_recv()
        z_copy(step, 1, step + 1).start()
        back = 8 - step
        z_copy((back + 1) % 8, -1, back).wait_recv()
        z_copy(back, -1, back - 1).start()
        to_sibling(0, step)
        to_sibling(0, back)

    def x_out(*dzs):
        for dz in dzs:
            x_copy(dz, 1).start()
            x_copy(dz, -1).start()

    def x_arrive(*dzs):
        for dz in dzs:
            for way in (1, -1):
                x_copy(dz, way).wait_recv()
                x_half(dz, way).start()
            for way in (1, -1):
                to_sibling(way % 4, dz)

    def far_arrive(*dzs):
        for dz in dzs:
            for way in (1, -1):
                x_half(dz, way).wait_recv()
            to_sibling(2, dz)

    def to_mine(d):
        to = mod(ja + d, 8)
        src = hop.at[mod(y - to // 2, 4), :, :, pl.ds(pl.multiple_of(lax.rem(to, 2) * COLS, COLS), COLS)]
        if d == 0:
            return pltpu.make_async_copy(src, mine.at[0], mine_recv.at[0])
        return remote(src, mine.at[d], mine_send.at[d], mine_recv.at[d], (ia, to, y))

    def to_hop(r, b):
        at = mod(y + r - z_hi * 2 - b - c, 4) * 2 + b
        if r == 0:
            return pltpu.make_async_copy(cots.at[at], hop.at[0, b], hop_recv.at[0, b])
        return remote(cots.at[at], hop.at[r, b], hop_send.at[r, b], hop_recv.at[r, b], device(dy=r))

    def cot_out():
        for r in range(4):
            for b in range(2):
                to_hop(r, b).wait_recv() if r else to_hop(r, b).wait()
        for d in range(8):
            to_mine(d).start()

    loads[0].wait()
    z_copy(0, 1, 1).start()
    z_copy(0, -1, 7).start()
    x_out(0)
    to_sibling(0, 0)
    loads[1].wait()
    for r in range(4):
        for b in range(2):
            to_hop(r, b).start()
    grad_ref[...] = jnp.zeros_like(grad_ref)
    loads[2].wait()

    events = {
        0: lambda: (z_arrive(1), x_out(1, 7), x_arrive(0), cot_out()),
        1: lambda: (z_arrive(2), x_out(2, 6)),
        2: lambda: (z_arrive(3),),
        3: lambda: (x_arrive(1, 7), x_out(3, 5), z_arrive(4)),
        4: lambda: (far_arrive(0),),
        6: lambda: (x_arrive(2, 6), x_out(4)),
        8: lambda: (far_arrive(1, 7),),
        9: lambda: (x_arrive(3, 5),),
        11: lambda: (far_arrive(2),),
        12: lambda: (x_arrive(4),),
        14: lambda: (far_arrive(3, 5),),
        15: lambda: (far_arrive(6, 4),),
    }

    def place(n, r):
        first = pick(n, [pair[0] for pair in OFF_Z])
        v = mod(y + r - x + pick(n, OFF_X) - z + first, 4)
        i = v // 2
        return i, lax.rem(v + c, 2)

    def rs_copy(n, r):
        i, k = place(n, r)
        return remote(pb.at[n, i, k], terms.at[n, r - 1], rs_send.at[n, r - 1], rs_recv.at[n, r - 1], device(dy=r))

    def ag_copy(n, r):
        i, k = place(n, 0)
        return remote(slopes.at[n, i, k], slopes.at[n, i, k], ag_send.at[n, r - 1], ag_recv.at[n, r - 1], device(dy=r))

    def source(n):
        i, k = place(n, 0)
        dz = jnp.where(i == 0, pick(n, [pair[0] for pair in OFF_Z]), pick(n, [pair[1] for pair in OFF_Z]))
        return mod(x - pick(n, OFF_X), 4), mod(z - dz, 8), lax.rem(c + k, 2)

    def act_copies(n):
        sx, sz, sc = source(n)
        at = sx * 2 + lax.rem(sz, 2)
        dst = act_ref.at[at, :, pl.ds(pl.multiple_of(c * COLS, COLS), COLS)]
        here = at_home & (sz // 2 == z_hi) & (sc == c)
        to = (ia, (sz // 2) * 2 + sc, z_hi)
        return (here, pltpu.make_async_copy(acts.at[n], dst, act_recv.at[at, c]),
                remote(acts.at[n], dst, act_send.at[n], act_recv.at[at, c], to))

    def forward(n):
        for i in range(2):
            sib_copy(n, i).wait_recv()
        out = jnp.dot(xs[n].reshape(4 * ROWS, DEPTH), ws[...], preferred_element_type=jnp.float32)
        pf[n] = out.reshape(2, 2, ROWS, COLS)
        pb[n] = out.astype(jnp.bfloat16).reshape(2, 2, ROWS, COLS)
        for r in (1, 3, 2):
            rs_copy(n, r).start()

    def middle(n):
        for r in (1, 3, 2):
            rs_copy(n, r).wait_recv()
        i, k = place(n, 0)
        _, sz, sc = source(n)
        pre = pf[n, i, k]
        for r in range(3):
            pre += terms[n, r].astype(jnp.float32)
        cot = mine[mod(ja - (sz // 2) * 2 - sc, 8), lax.rem(sz, 2)].astype(jnp.float32)
        root = 0.7978845608028654
        square = pre * pre
        t = jnp.tanh(root * pre * (1.0 + 0.044715 * square))
        slope = 0.5 * (1.0 + t) + 0.5 * pre * (1.0 - t * t) * (root * (1.0 + 3 * 0.044715 * square))
        slopes[n, i, k] = (cot * slope).astype(jnp.bfloat16)
        for r in (1, 3, 2):
            ag_copy(n, r).start()
        acts[n] = (0.5 * pre * (1.0 + t)).astype(jnp.bfloat16)
        here, local_copy, remote_copy = act_copies(n)
        pl.when(here)(local_copy.start)
        pl.when(jnp.logical_not(here))(remote_copy.start)

    def backward(n):
        for r in (1, 3, 2):
            ag_copy(n, r).wait_recv()
        s = slopes[n].reshape(4 * ROWS, COLS)
        for b in range(4):
            cols = pl.ds(b * 512, 512)
            grad_ref[cols, :] += lax.dot_general(
                xs[n, :, :, :, cols].reshape(4 * ROWS, 512), s, (((0,), (0,)), ((), ())),
                preferred_element_type=jnp.float32)

    def step(n, carry):
        for at, event in events.items():
            pl.when(n == at)(lambda event=event: (event(), None)[1])
        pl.when(n < CHUNKS)(lambda: forward(n))

        @pl.when(n == 1)
        def _():
            for d in range(8):
                to_mine(d).wait_recv() if d else to_mine(d).wait()

        pl.when((n >= 1) & (n < CHUNKS + 1))(lambda: middle(n - 1))
        pl.when(n >= GRAD_LAG)(lambda: backward(n - GRAD_LAG))
        return carry

    lax.fori_loop(0, CHUNKS + GRAD_LAG, step, 0)

    for at in range(8):
        for core in range(2):
            dst = act_ref.at[at, :, pl.ds(core * COLS, COLS)]
            pltpu.make_async_copy(acts.at[0], dst, act_recv.at[at, core]).wait()
    for dz, way, dst in ((0, 1, 1), (1, 1, 2), (2, 1, 3), (3, 1, 4), (0, -1, 7), (7, -1, 6), (6, -1, 5), (5, -1, 4)):
        z_copy(dz, way, dst).wait_send()
    for dz in range(8):
        for way in (1, -1):
            x_copy(dz, way).wait_send()
            x_half(dz, way).wait_send()
    for r in range(1, 4):
        for b in range(2):
            to_hop(r, b).wait_send()
    for d in range(1, 8):
        to_mine(d).wait_send()

    def drain(n, carry):
        for i in range(2):
            sib_copy(n, i).wait_send()
        for r in (1, 2, 3):
            rs_copy(n, r).wait_send()
            ag_copy(n, r).wait_send()
        here, _, remote_copy = act_copies(n)
        pl.when(jnp.logical_not(here))(remote_copy.wait_send)
        return carry

    lax.fori_loop(0, CHUNKS, drain, 0)


def local(tokens, weight_up, cotangent):
    dma = pltpu.SemaphoreType.DMA
    bf16, f32 = jnp.bfloat16, jnp.float32
    act, grad = pl.pallas_call(
        kernel,
        name="mlp_up",
        out_shape=(jax.ShapeDtypeStruct((8, ROWS, 2 * COLS), bf16), jax.ShapeDtypeStruct((DEPTH, COLS), f32)),
        in_specs=[pl.BlockSpec(memory_space=pl.ANY)] * 3,
        out_specs=(pl.BlockSpec(memory_space=pltpu.VMEM),) * 2,
        scratch_shapes=[
            pltpu.VMEM((CHUNKS, 2, 2, ROWS, DEPTH), bf16),
            pltpu.VMEM((DEPTH, COLS), bf16),
            pltpu.VMEM((8, ROWS, 2 * COLS), bf16),
            pltpu.VMEM((4, 2, ROWS, 2 * COLS), bf16),
            pltpu.VMEM((8, 2, ROWS, COLS), bf16),
            pltpu.VMEM((CHUNKS, 2, 2, ROWS, COLS), f32),
            pltpu.VMEM((CHUNKS, 2, 2, ROWS, COLS), bf16),
            pltpu.VMEM((CHUNKS, 3, ROWS, COLS), bf16),
            pltpu.VMEM((CHUNKS, 2, 2, ROWS, COLS), bf16),
            pltpu.VMEM((CHUNKS, ROWS, COLS), bf16),
            dma((3,)),
            dma((8,)), dma((8,)),
            dma((4, 8)), dma((4, 8)),
            dma((CHUNKS, 2)), dma((CHUNKS, 2)),
            dma((CHUNKS, 3)), dma((CHUNKS, 3)),
            dma((CHUNKS, 3)), dma((CHUNKS, 3)),
            dma((4, 2)), dma((4, 2)),
            dma((8,)), dma((8,)),
            dma((CHUNKS,)), dma((8, 2)),
        ],
        compiler_params=pltpu.CompilerParams(
            collective_id=0, has_side_effects=True, vmem_limit_bytes=56 << 20),
    )(tokens.reshape(ROWS, DEPTH), weight_up, cotangent.reshape(8, ROWS, 2 * COLS))
    return act.reshape(1, 8 * ROWS, 2 * COLS), grad


def solution(mesh):
    return jax.shard_map(
        local,
        mesh=mesh,
        in_specs=(P("ja", "ia", "ka"), P("ka", ("ia", "ja")), P("ja", None, ("ia", "ka"))),
        out_specs=(P("ja", None, ("ia", "ka")), P("ka", ("ia", "ja"))),
        check_vma=False,
    )
```

```python
import jax
import jax.numpy as jnp
from jax import lax
from jax.experimental import pallas as pl
from jax.experimental.pallas import tpu as pltpu
from jax.sharding import PartitionSpec as P

MESH = pl.DeviceIdType.MESH
ROWS, DEPTH, COLS = 48, 2048, 384
HALF = DEPTH // 2
PAIRS = ((1, 7), (0, 2), (3, 5), (6, 4))
ORDER = (
    (0, 0), (0, 1), (1, 0), (3, 0), (0, 2), (1, 1), (3, 1), (2, 0),
    (0, 3), (1, 2), (3, 2), (2, 1), (1, 3), (3, 3), (2, 2), (2, 3),
)
CHUNKS = len(ORDER)
SLOT = {(dx, dz): (n, i) for n, (dx, p) in enumerate(ORDER) for i, dz in enumerate(PAIRS[p])}
OFF_X = tuple(dx for dx, _ in ORDER)
OFF_Z = tuple(PAIRS[p] for _, p in ORDER)
SCHEDULE = (
    ((("z", 1), ("z", 7), ("x", 0), ("x_out", 1, 7)), 0, 0, 0),
    ((("near",), ("far", 0), ("z", 2), ("z", 6), ("x_out", 2, 6)), 0, 1, 0),
    ((("x", 1),), 1, -1, 0),
    ((("x", 7),), 2, 2, 0),
    ((("relay", 0),), 2, 3, 0),
    ((("z", 3), ("z", 5), ("x", 2), ("x_out", 3, 5), ("relay", 1)), 3, 4, 0),
    ((), 3, 5, 0),
    ((("z", 4), ("x", 6), ("x_out", 4), ("cot_far",)), 4, -1, 0),
    ((("relay", 2),), 4, 6, 0),
    ((("far", 1),), 4, -1, 2),
    ((("far", 7), ("relay", 3)), 4, 7, 2),
    ((("far", 2),), 4, 8, 3),
    ((), 7, -1, 3),
    ((("x", 3),), 8, -1, 4),
    ((("relay", 4),), 9, -1, 4),
    ((("relay", 5), ("x", 5), ("relay", 6), ("relay", 7)), 9, 9, 4),
    ((("far", 6),), 9, 10, 4),
    ((("relay", 8),), 9, 11, 6),
    ((("x", 4),), 11, -1, 7),
    ((("far", 3),), 11, 12, 7),
    ((("relay", 9), ("far", 5)), 12, 13, 7),
    ((("relay", 10),), 12, 14, 7),
    ((("far", 4),), 12, -1, 8),
    ((), 13, 15, 8),
    ((("relay", 11),), 13, -1, 9),
    ((), 14, -1, 11),
    ((("relay", 12),), 16, -1, 12),
    ((("relay", 13),), 16, -1, 13),
    ((("relay", 14), ("relay", 15)), 16, -1, 16),
)


def pick(index, table):
    out = jnp.int32(table[0])
    for j, entry in enumerate(table[1:], 1):
        out = jnp.where(index == j, jnp.int32(entry), out)
    return out


def mod(value, n):
    return lax.rem(value + 16 * n, n)


def kernel(tok_ref, w_ref, cot_ref, act_ref, grad_ref, xs, ws, cots, hop, mine, pf, pb, terms, slopes, acts,
           load_sem, z_send, z_recv, x_send, x_recv, sib_send, sib_recv, rs_send, rs_recv, ag_send, ag_recv,
           hop_send, hop_recv, mine_send, mine_recv, act_send, act_recv):
    ia, ja, y = lax.axis_index("ia"), lax.axis_index("ja"), lax.axis_index("ka")
    x, z_lo, z_hi, c = ia // 2, lax.rem(ia, 2), ja // 2, lax.rem(ja, 2)
    z = z_hi * 2 + z_lo

    def device(dx=0, dz=0, dy=0):
        tz = mod(z + dz, 8)
        return (mod(x + dx, 4) * 2 + lax.rem(tz, 2), (tz // 2) * 2 + c, mod(y + dy, 4))

    sibling = (ia, z_hi * 2 + 1 - c, y)

    def remote(src, dst, send, recv, to):
        return pltpu.make_async_remote_copy(
            src_ref=src, dst_ref=dst, send_sem=send, recv_sem=recv, device_id=to, device_id_type=MESH)

    loads = [
        pltpu.make_async_copy(tok_ref, xs.at[SLOT[0, 0][0], SLOT[0, 0][1], 0], load_sem.at[0]),
        pltpu.make_async_copy(cot_ref, cots, load_sem.at[1]),
        pltpu.make_async_copy(w_ref, ws, load_sem.at[2]),
    ]
    for load in loads:
        load.start()

    barrier = pltpu.get_barrier_semaphore()
    for to in [device(dx=1), device(dx=-1), device(dz=1), device(dz=-1)] + [device(dy=r) for r in (1, 2, 3)] + [
            (ia, mod(ja + d, 8), y) for d in range(1, 8)]:
        pl.semaphore_signal(barrier, inc=1, device_id=to, device_id_type=MESH)
    at_home = y == z_hi
    for owner in range(4):
        for core in range(2):
            @pl.when(jnp.logical_not(at_home & (owner == y) & (core == c)))
            def _():
                pl.semaphore_signal(barrier, inc=1, device_id=(ia, y * 2 + core, owner), device_id_type=MESH)
    pl.semaphore_wait(barrier, 14 + 8 - jnp.where(at_home, 1, 0))

    def block(dx, dz, core=0):
        n, i = SLOT[dx, dz]
        return xs.at[n, i, core]

    def half(ref, h):
        return ref.at[:, pl.ds(h * HALF, HALF)]

    def z_copy(dz, way, dst_dz):
        src = block(0, dz)
        if dst_dz == 4:
            h = 0 if way == 1 else 1
            return remote(half(src, h), half(block(0, 4), h), z_send.at[h * 4], z_recv.at[h * 4], device(dz=way))
        return remote(src, block(0, dst_dz), z_send.at[dst_dz], z_recv.at[dst_dz], device(dz=way))

    def x_copy(dz, way):
        dx = way % 4
        return remote(block(0, dz), block(dx, dz), x_send.at[dx, dz], x_recv.at[dx, dz], device(dx=way))

    def x_half(dz, way):
        h = 0 if way == 1 else 1
        return remote(half(block(way % 4, dz), h), half(block(2, dz), h), x_send.at[h * 2, dz], x_recv.at[h * 2, dz],
                      device(dx=way))

    def sib_copy(n, i):
        return remote(xs.at[n, i, 0], xs.at[n, i, 1], sib_send.at[n, i], sib_recv.at[n, i], sibling)

    def to_sibling(dx, dz):
        sib_copy(*SLOT[dx, dz]).start()

    def z_arrive(*dzs):
        for dz in dzs:
            if dz == 4:
                z_copy(3, 1, 4).wait_recv()
                z_copy(5, -1, 4).wait_recv()
            else:
                way = 1 if dz < 4 else -1
                z_copy((dz - way) % 8, way, dz).wait_recv()
                z_copy(dz, way, dz + way).start()
        for dz in dzs:
            to_sibling(0, dz)

    def x_out(*dzs):
        for dz in dzs:
            x_copy(dz, 1).start()
            x_copy(dz, -1).start()

    def x_arrive(*dzs):
        for dz in dzs:
            for way in (1, -1):
                x_copy(dz, way).wait_recv()
                x_half(dz, way).start()
            for way in (1, -1):
                to_sibling(way % 4, dz)

    def far_arrive(*dzs):
        for dz in dzs:
            for way in (1, -1):
                x_half(dz, way).wait_recv()
            to_sibling(2, dz)

    def to_mine(dz, other, b):
        tz, tc = mod(z_hi + dz, 4), (1 - c if other else c)
        src = hop.at[mod(y - tz, 4), b, :, pl.ds(pl.multiple_of(tc * COLS, COLS), COLS)]
        d = dz * 2 + other
        if d == 0:
            return pltpu.make_async_copy(src, mine.at[0, b], mine_recv.at[0, b])
        return remote(src, mine.at[d, b], mine_send.at[d, b], mine_recv.at[d, b], (ia, tz * 2 + tc, y))

    def to_hop(r, b):
        at = mod(y + r - z_hi * 2 - b - c, 4) * 2 + b
        if r == 0:
            return pltpu.make_async_copy(cots.at[at], hop.at[0, b], hop_recv.at[0, b])
        return remote(cots.at[at], hop.at[r, b], hop_send.at[r, b], hop_recv.at[r, b], device(dy=r))

    def cot_near():
        for r in range(4):
            for b in range(2):
                to_hop(r, b).wait_recv() if r else to_hop(r, b).wait()
        for dz in (0, 1, 3):
            for other in (0, 1):
                for b in range(2):
                    to_mine(dz, other, b).start()

    def cot_far():
        for other in (0, 1):
            for b in range(2):
                to_mine(2, other, b).start()

    loads[0].wait()
    z_copy(0, 1, 1).start()
    z_copy(0, -1, 7).start()
    x_out(0)
    to_sibling(0, 0)
    loads[1].wait()
    for r in range(4):
        for b in range(2):
            to_hop(r, b).start()
    grad_ref[...] = jnp.zeros_like(grad_ref)
    loads[2].wait()

    def place(n, r):
        first = pick(n, [pair[0] for pair in OFF_Z])
        v = mod(y + r - x + pick(n, OFF_X) - z + first, 4)
        i = v // 2
        return i, lax.rem(v + c, 2)

    def rs_copy(n, r):
        i, k = place(n, r)
        return remote(pb.at[n, i, k], terms.at[n, r - 1], rs_send.at[n, r - 1], rs_recv.at[n, r - 1], device(dy=r))

    def ag_copy(n, way):
        i, k = place(n, 0)
        return remote(slopes.at[n, i, k], slopes.at[n, i, k], ag_send.at[n, way - 1], ag_recv.at[n, way - 1],
                      device(dy=way))

    def ag_second(n):
        way = 1 + 2 * lax.rem(n, 2)
        i, k = place(n, 4 - way)
        return remote(slopes.at[n, i, k], slopes.at[n, i, k], ag_send.at[n, 1], ag_recv.at[n, 1], device(dy=way))

    def relay(n):
        ag_copy(n, 1 + 2 * (n % 2)).wait_recv()
        ag_second(n).start()

    def source(n):
        i, k = place(n, 0)
        dz = jnp.where(i == 0, pick(n, [pair[0] for pair in OFF_Z]), pick(n, [pair[1] for pair in OFF_Z]))
        return mod(x - pick(n, OFF_X), 4), mod(z - dz, 8), lax.rem(c + k, 2)

    def act_copies(n):
        sx, sz, sc = source(n)
        at = sx * 2 + lax.rem(sz, 2)
        dst = act_ref.at[at, :, pl.ds(pl.multiple_of(c * COLS, COLS), COLS)]
        here = at_home & (sz // 2 == z_hi) & (sc == c)
        to = (ia, (sz // 2) * 2 + sc, z_hi)
        return (here, pltpu.make_async_copy(acts.at[n], dst, act_recv.at[at, c]),
                remote(acts.at[n], dst, act_send.at[n], act_recv.at[at, c], to))

    def forward(n):
        for i in range(2):
            sib_copy(n, i).wait_recv()
        out = jnp.dot(xs[n].reshape(4 * ROWS, DEPTH), ws[...], preferred_element_type=jnp.float32)
        pf[n] = out.reshape(2, 2, ROWS, COLS)
        pb[n] = out.astype(jnp.bfloat16).reshape(2, 2, ROWS, COLS)
        for r in (1, 3, 2):
            rs_copy(n, r).start()

    def middle(n):
        for r in (1, 3, 2):
            rs_copy(n, r).wait_recv()
        i, k = place(n, 0)
        _, sz, sc = source(n)
        pre = pf[n, i, k]
        for r in range(3):
            pre += terms[n, r].astype(jnp.float32)
        d, b = mod(z_hi - sz // 2, 4) * 2 + lax.rem(sc + c, 2), lax.rem(sz, 2)
        pltpu.make_async_copy(mine.at[d, b], mine.at[d, b], mine_recv.at[d, b]).wait()
        cot = mine[d, b].astype(jnp.float32)
        root = 0.7978845608028654
        square = pre * pre
        t = jnp.tanh(root * pre * (1.0 + 0.044715 * square))
        slope = 0.5 * (1.0 + t) + 0.5 * pre * (1.0 - t * t) * (root * (1.0 + 3 * 0.044715 * square))
        slopes[n, i, k] = (cot * slope).astype(jnp.bfloat16)
        for r in (1, 3):
            ag_copy(n, r).start()
        acts[n] = (0.5 * pre * (1.0 + t)).astype(jnp.bfloat16)
        here, local_copy, remote_copy = act_copies(n)
        pl.when(here)(local_copy.start)
        pl.when(jnp.logical_not(here))(remote_copy.start)

    def backward(n):
        ag_copy(n, 3 - 2 * lax.rem(n, 2)).wait_recv()
        ag_second(n).wait_recv()
        s = slopes[n].reshape(4 * ROWS, COLS)
        for b in range(4):
            cols = pl.ds(b * 512, 512)
            grad_ref[cols, :] += lax.dot_general(
                xs[n, :, :, :, cols].reshape(4 * ROWS, 512), s, (((0,), (0,)), ((), ())),
                preferred_element_type=jnp.float32)

    actions = {
        "z": z_arrive, "x_out": x_out, "x": x_arrive, "far": far_arrive,
        "near": cot_near, "cot_far": cot_far, "relay": relay,
    }
    mids, grads = [0], [0]
    for _, mid, _, grad in SCHEDULE:
        mids.append(mid)
        grads.append(grad)

    def step(t, carry):
        for at, (events, _, chunk, _) in enumerate(SCHEDULE):
            if events:
                @pl.when(t == at)
                def _():
                    for name, *args in events:
                        actions[name](*args)
        lax.fori_loop(pick(t, mids), pick(t, mids[1:]), lambda n, _: (middle(n), 0)[1], 0)
        chunk = pick(t, [entry[2] for entry in SCHEDULE])
        pl.when(chunk >= 0)(lambda: forward(chunk))
        lax.fori_loop(pick(t, grads), pick(t, grads[1:]), lambda n, _: (backward(n), 0)[1], 0)
        return carry

    lax.fori_loop(0, len(SCHEDULE), step, 0)

    for at in range(8):
        for core in range(2):
            dst = act_ref.at[at, :, pl.ds(core * COLS, COLS)]
            pltpu.make_async_copy(acts.at[0], dst, act_recv.at[at, core]).wait()
    for dz, way, dst in ((0, 1, 1), (1, 1, 2), (2, 1, 3), (3, 1, 4), (0, -1, 7), (7, -1, 6), (6, -1, 5), (5, -1, 4)):
        z_copy(dz, way, dst).wait_send()
    for dz in range(8):
        for way in (1, -1):
            x_copy(dz, way).wait_send()
            x_half(dz, way).wait_send()
    for r in range(1, 4):
        for b in range(2):
            to_hop(r, b).wait_send()
    for d in range(2, 16):
        to_mine(d // 4, d // 2 % 2, d % 2).wait_send()

    def drain(n, carry):
        for i in range(2):
            sib_copy(n, i).wait_send()
        for r in (1, 2, 3):
            rs_copy(n, r).wait_send()
        for way in (1, 3):
            ag_copy(n, way).wait_send()
        ag_second(n).wait_send()
        here, _, remote_copy = act_copies(n)
        pl.when(jnp.logical_not(here))(remote_copy.wait_send)
        return carry

    lax.fori_loop(0, CHUNKS, drain, 0)


def local(tokens, weight_up, cotangent):
    dma = pltpu.SemaphoreType.DMA
    bf16, f32 = jnp.bfloat16, jnp.float32
    act, grad = pl.pallas_call(
        kernel,
        name="mlp_up",
        out_shape=(jax.ShapeDtypeStruct((8, ROWS, 2 * COLS), bf16), jax.ShapeDtypeStruct((DEPTH, COLS), f32)),
        in_specs=[pl.BlockSpec(memory_space=pl.ANY)] * 3,
        out_specs=(pl.BlockSpec(memory_space=pltpu.VMEM),) * 2,
        scratch_shapes=[
            pltpu.VMEM((CHUNKS, 2, 2, ROWS, DEPTH), bf16),
            pltpu.VMEM((DEPTH, COLS), bf16),
            pltpu.VMEM((8, ROWS, 2 * COLS), bf16),
            pltpu.VMEM((4, 2, ROWS, 2 * COLS), bf16),
            pltpu.VMEM((8, 2, ROWS, COLS), bf16),
            pltpu.VMEM((CHUNKS, 2, 2, ROWS, COLS), f32),
            pltpu.VMEM((CHUNKS, 2, 2, ROWS, COLS), bf16),
            pltpu.VMEM((CHUNKS, 3, ROWS, COLS), bf16),
            pltpu.VMEM((CHUNKS, 2, 2, ROWS, COLS), bf16),
            pltpu.VMEM((CHUNKS, ROWS, COLS), bf16),
            dma((3,)),
            dma((8,)), dma((8,)),
            dma((4, 8)), dma((4, 8)),
            dma((CHUNKS, 2)), dma((CHUNKS, 2)),
            dma((CHUNKS, 3)), dma((CHUNKS, 3)),
            dma((CHUNKS, 3)), dma((CHUNKS, 3)),
            dma((4, 2)), dma((4, 2)),
            dma((8, 2)), dma((8, 2)),
            dma((CHUNKS,)), dma((8, 2)),
        ],
        compiler_params=pltpu.CompilerParams(
            collective_id=0, has_side_effects=True, vmem_limit_bytes=56 << 20),
    )(tokens.reshape(ROWS, DEPTH), weight_up, cotangent.reshape(8, ROWS, 2 * COLS))
    return act.reshape(1, 8 * ROWS, 2 * COLS), grad


def solution(mesh):
    return jax.shard_map(
        local,
        mesh=mesh,
        in_specs=(P("ja", "ia", "ka"), P("ka", ("ia", "ja")), P("ja", None, ("ia", "ka"))),
        out_specs=(P("ja", None, ("ia", "ka")), P("ka", ("ia", "ja"))),
        check_vma=False,
    )
```

```python
import jax
import jax.numpy as jnp
from jax import lax
from jax.experimental import pallas as pl
from jax.experimental.pallas import tpu as pltpu
from jax.sharding import PartitionSpec as P

MESH = pl.DeviceIdType.MESH
ROWS, DEPTH, COLS = 48, 2048, 384
HALF = DEPTH // 2
PAIRS = ((1, 7), (0, 2), (3, 5), (6, 4))
ORDER = (
    (0, 0), (0, 1), (1, 0), (3, 0), (0, 2), (1, 1), (3, 1), (2, 0),
    (0, 3), (1, 2), (3, 2), (2, 1), (1, 3), (3, 3), (2, 2), (2, 3),
)
CHUNKS = len(ORDER)
SLOT = {(dx, dz): (n, i) for n, (dx, p) in enumerate(ORDER) for i, dz in enumerate(PAIRS[p])}
OFF_X = tuple(dx for dx, _ in ORDER)
OFF_Z = tuple(PAIRS[p] for _, p in ORDER)
SCHEDULE = (
    ((("z", 1), ("z", 7), ("x", 0), ("x_out", 1, 7)), 0, 0, 0),
    ((("near",), ("far", 0), ("z", 2), ("z", 6), ("x_out", 2, 6)), 0, 1, 0),
    ((("x", 1),), 1, -1, 0),
    ((("x", 7),), 2, 2, 0),
    ((), 2, 3, 0),
    ((("z", 3), ("z", 5), ("x", 2), ("x_out", 3, 5), ("relay", 0), ("relay", 1)), 2, 4, 0),
    ((), 3, 5, 0),
    ((("x", 6), ("z", 4), ("x_out", 4), ("cot_far",)), 4, 6, 0),
    ((("far", 1),), 4, -1, 2),
    ((("far", 7), ("relay", 2), ("far", 2)), 4, 7, 2),
    ((("relay", 3),), 4, 8, 3),
    ((("x", 3),), 8, -1, 4),
    ((), 9, -1, 4),
    ((("x", 5), ("relay", 4)), 9, 9, 4),
    ((("far", 6), ("relay", 5), ("relay", 6)), 9, 10, 4),
    ((), 9, 11, 4),
    ((("relay", 7), ("relay", 8), ("x", 4)), 9, -1, 5),
    ((), 9, 12, 5),
    ((("far", 3),), 10, 13, 5),
    ((("far", 5),), 11, -1, 6),
    ((), 12, -1, 6),
    ((("far", 4),), 12, 14, 7),
    ((("relay", 9),), 13, 15, 8),
    ((), 14, -1, 8),
    ((("relay", 10), ("relay", 11)), 14, -1, 9),
    ((), 15, -1, 10),
    ((("relay", 12),), 16, -1, 10),
    ((("relay", 13),), 16, -1, 11),
    ((("relay", 14),), 16, -1, 12),
    ((("relay", 15),), 16, -1, 16),
)


def pick(index, table):
    out = jnp.int32(table[0])
    for j, entry in enumerate(table[1:], 1):
        out = jnp.where(index == j, jnp.int32(entry), out)
    return out


def mod(value, n):
    return lax.rem(value + 16 * n, n)


def kernel(tok_ref, w_ref, cot_ref, act_ref, grad_ref, xs, ws, cots, hop, mine, pf, pb, terms, slopes, acts,
           load_sem, z_send, z_recv, x_send, x_recv, sib_send, sib_recv, rs_send, rs_recv, ag_send, ag_recv,
           hop_send, hop_recv, mine_send, mine_recv, act_send, act_recv):
    ia, ja, y = lax.axis_index("ia"), lax.axis_index("ja"), lax.axis_index("ka")
    x, z_lo, z_hi, c = ia // 2, lax.rem(ia, 2), ja // 2, lax.rem(ja, 2)
    z = z_hi * 2 + z_lo

    def device(dx=0, dz=0, dy=0):
        tz = mod(z + dz, 8)
        return (mod(x + dx, 4) * 2 + lax.rem(tz, 2), (tz // 2) * 2 + c, mod(y + dy, 4))

    sibling = (ia, z_hi * 2 + 1 - c, y)

    def remote(src, dst, send, recv, to):
        return pltpu.make_async_remote_copy(
            src_ref=src, dst_ref=dst, send_sem=send, recv_sem=recv, device_id=to, device_id_type=MESH)

    loads = [
        pltpu.make_async_copy(tok_ref, xs.at[SLOT[0, 0][0], SLOT[0, 0][1], 0], load_sem.at[0]),
        pltpu.make_async_copy(cot_ref, cots, load_sem.at[1]),
        pltpu.make_async_copy(w_ref, ws, load_sem.at[2]),
    ]
    for load in loads:
        load.start()

    barrier = pltpu.get_barrier_semaphore()
    for to in [device(dx=1), device(dx=-1), device(dz=1), device(dz=-1)] + [device(dy=r) for r in (1, 2, 3)] + [
            (ia, mod(ja + d, 8), y) for d in range(1, 8)]:
        pl.semaphore_signal(barrier, inc=1, device_id=to, device_id_type=MESH)
    at_home = y == z_hi
    for owner in range(4):
        for core in range(2):
            @pl.when(jnp.logical_not(at_home & (owner == y) & (core == c)))
            def _():
                pl.semaphore_signal(barrier, inc=1, device_id=(ia, y * 2 + core, owner), device_id_type=MESH)
    pl.semaphore_wait(barrier, 14 + 8 - jnp.where(at_home, 1, 0))

    def block(dx, dz, core=0):
        n, i = SLOT[dx, dz]
        return xs.at[n, i, core]

    def half(ref, h):
        return ref.at[:, pl.ds(h * HALF, HALF)]

    def z_copy(dz, way, dst_dz):
        src = block(0, dz)
        if dst_dz == 4:
            h = 0 if way == 1 else 1
            return remote(half(src, h), half(block(0, 4), h), z_send.at[h * 4], z_recv.at[h * 4], device(dz=way))
        return remote(src, block(0, dst_dz), z_send.at[dst_dz], z_recv.at[dst_dz], device(dz=way))

    def x_copy(dz, way):
        dx = way % 4
        return remote(block(0, dz), block(dx, dz), x_send.at[dx, dz], x_recv.at[dx, dz], device(dx=way))

    def x_half(dz, way):
        h = 0 if way == 1 else 1
        return remote(half(block(way % 4, dz), h), half(block(2, dz), h), x_send.at[h * 2, dz], x_recv.at[h * 2, dz],
                      device(dx=way))

    def sib_copy(n, i):
        return remote(xs.at[n, i, 0], xs.at[n, i, 1], sib_send.at[n, i], sib_recv.at[n, i], sibling)

    def to_sibling(dx, dz):
        sib_copy(*SLOT[dx, dz]).start()

    def z_arrive(*dzs):
        for dz in dzs:
            if dz == 4:
                z_copy(3, 1, 4).wait_recv()
                z_copy(5, -1, 4).wait_recv()
            else:
                way = 1 if dz < 4 else -1
                z_copy((dz - way) % 8, way, dz).wait_recv()
                z_copy(dz, way, dz + way).start()
        for dz in dzs:
            to_sibling(0, dz)

    def x_out(*dzs):
        for dz in dzs:
            x_copy(dz, 1).start()
            x_copy(dz, -1).start()

    def x_arrive(*dzs):
        for dz in dzs:
            for way in (1, -1):
                x_copy(dz, way).wait_recv()
                x_half(dz, way).start()
            for way in (1, -1):
                to_sibling(way % 4, dz)

    def far_arrive(*dzs):
        for dz in dzs:
            for way in (1, -1):
                x_half(dz, way).wait_recv()
            to_sibling(2, dz)

    def to_mine(dz, other, b):
        tz, tc = mod(z_hi + dz, 4), (1 - c if other else c)
        src = hop.at[mod(y - tz, 4), b, :, pl.ds(pl.multiple_of(tc * COLS, COLS), COLS)]
        d = dz * 2 + other
        if d == 0:
            return pltpu.make_async_copy(src, mine.at[0, b], mine_recv.at[0, b])
        return remote(src, mine.at[d, b], mine_send.at[d, b], mine_recv.at[d, b], (ia, tz * 2 + tc, y))

    def to_hop(r, b):
        at = mod(y + r - z_hi * 2 - b - c, 4) * 2 + b
        if r == 0:
            return pltpu.make_async_copy(cots.at[at], hop.at[0, b], hop_recv.at[0, b])
        return remote(cots.at[at], hop.at[r, b], hop_send.at[r, b], hop_recv.at[r, b], device(dy=r))

    def cot_near():
        for r in range(4):
            for b in range(2):
                to_hop(r, b).wait_recv() if r else to_hop(r, b).wait()
        for dz in (0, 1, 3):
            for other in (0, 1):
                for b in range(2):
                    to_mine(dz, other, b).start()

    def cot_far():
        for other in (0, 1):
            for b in range(2):
                to_mine(2, other, b).start()

    loads[0].wait()
    z_copy(0, 1, 1).start()
    z_copy(0, -1, 7).start()
    x_out(0)
    to_sibling(0, 0)
    loads[1].wait()
    for r in range(4):
        for b in range(2):
            to_hop(r, b).start()
    grad_ref[...] = jnp.zeros_like(grad_ref)
    loads[2].wait()

    def place(n, r):
        first = pick(n, [pair[0] for pair in OFF_Z])
        v = mod(y + r - x + pick(n, OFF_X) - z + first, 4)
        i = v // 2
        return i, lax.rem(v + c, 2)

    def rs_copy(n, r):
        i, k = place(n, r)
        return remote(pb.at[n, i, k], terms.at[n, r - 1], rs_send.at[n, r - 1], rs_recv.at[n, r - 1], device(dy=r))

    def ag_copy(n, way):
        i, k = place(n, 0)
        return remote(slopes.at[n, i, k], slopes.at[n, i, k], ag_send.at[n, way - 1], ag_recv.at[n, way - 1],
                      device(dy=way))

    def ag_second(n):
        way = 1 + 2 * lax.rem(n, 2)
        i, k = place(n, 4 - way)
        return remote(slopes.at[n, i, k], slopes.at[n, i, k], ag_send.at[n, 1], ag_recv.at[n, 1], device(dy=way))

    def relay(n):
        ag_copy(n, 1 + 2 * (n % 2)).wait_recv()
        ag_second(n).start()

    def source(n):
        i, k = place(n, 0)
        dz = jnp.where(i == 0, pick(n, [pair[0] for pair in OFF_Z]), pick(n, [pair[1] for pair in OFF_Z]))
        return mod(x - pick(n, OFF_X), 4), mod(z - dz, 8), lax.rem(c + k, 2)

    def act_copies(n):
        sx, sz, sc = source(n)
        at = sx * 2 + lax.rem(sz, 2)
        dst = act_ref.at[at, :, pl.ds(pl.multiple_of(c * COLS, COLS), COLS)]
        here = at_home & (sz // 2 == z_hi) & (sc == c)
        to = (ia, (sz // 2) * 2 + sc, z_hi)
        return (here, pltpu.make_async_copy(acts.at[n], dst, act_recv.at[at, c]),
                remote(acts.at[n], dst, act_send.at[n], act_recv.at[at, c], to))

    def forward(n):
        for i in range(2):
            sib_copy(n, i).wait_recv()
        out = jnp.dot(xs[n].reshape(4 * ROWS, DEPTH), ws[...], preferred_element_type=jnp.float32)
        pf[n] = out.reshape(2, 2, ROWS, COLS)
        pb[n] = out.astype(jnp.bfloat16).reshape(2, 2, ROWS, COLS)
        for r in (1, 3, 2):
            rs_copy(n, r).start()

    def middle(n):
        for r in (1, 3, 2):
            rs_copy(n, r).wait_recv()
        i, k = place(n, 0)
        _, sz, sc = source(n)
        pre = pf[n, i, k]
        for r in range(3):
            pre += terms[n, r].astype(jnp.float32)
        d, b = mod(z_hi - sz // 2, 4) * 2 + lax.rem(sc + c, 2), lax.rem(sz, 2)
        pltpu.make_async_copy(mine.at[d, b], mine.at[d, b], mine_recv.at[d, b]).wait()
        cot = mine[d, b].astype(jnp.float32)
        root = 0.7978845608028654
        square = pre * pre
        t = jnp.tanh(root * pre * (1.0 + 0.044715 * square))
        slope = 0.5 * (1.0 + t) + 0.5 * pre * (1.0 - t * t) * (root * (1.0 + 3 * 0.044715 * square))
        slopes[n, i, k] = (cot * slope).astype(jnp.bfloat16)
        for r in (1, 3):
            ag_copy(n, r).start()
        acts[n] = (0.5 * pre * (1.0 + t)).astype(jnp.bfloat16)
        here, local_copy, remote_copy = act_copies(n)
        pl.when(here)(local_copy.start)
        pl.when(jnp.logical_not(here))(remote_copy.start)

    def backward(n):
        ag_copy(n, 3 - 2 * lax.rem(n, 2)).wait_recv()
        ag_second(n).wait_recv()
        s = slopes[n].reshape(4 * ROWS, COLS)
        for b in range(4):
            cols = pl.ds(b * 512, 512)
            grad_ref[cols, :] += lax.dot_general(
                xs[n, :, :, :, cols].reshape(4 * ROWS, 512), s, (((0,), (0,)), ((), ())),
                preferred_element_type=jnp.float32)

    actions = {
        "z": z_arrive, "x_out": x_out, "x": x_arrive, "far": far_arrive,
        "near": cot_near, "cot_far": cot_far, "relay": relay,
    }
    mids, grads = [0], [0]
    for _, mid, _, grad in SCHEDULE:
        mids.append(mid)
        grads.append(grad)

    def step(t, carry):
        for at, (events, _, chunk, _) in enumerate(SCHEDULE):
            if events:
                @pl.when(t == at)
                def _():
                    for name, *args in events:
                        actions[name](*args)
        lax.fori_loop(pick(t, mids), pick(t, mids[1:]), lambda n, _: (middle(n), 0)[1], 0)
        chunk = pick(t, [entry[2] for entry in SCHEDULE])
        pl.when(chunk >= 0)(lambda: forward(chunk))
        lax.fori_loop(pick(t, grads), pick(t, grads[1:]), lambda n, _: (backward(n), 0)[1], 0)
        return carry

    lax.fori_loop(0, len(SCHEDULE), step, 0)

    for at in range(8):
        for core in range(2):
            dst = act_ref.at[at, :, pl.ds(core * COLS, COLS)]
            pltpu.make_async_copy(acts.at[0], dst, act_recv.at[at, core]).wait()
    for dz, way, dst in ((0, 1, 1), (1, 1, 2), (2, 1, 3), (3, 1, 4), (0, -1, 7), (7, -1, 6), (6, -1, 5), (5, -1, 4)):
        z_copy(dz, way, dst).wait_send()
    for dz in range(8):
        for way in (1, -1):
            x_copy(dz, way).wait_send()
            x_half(dz, way).wait_send()
    for r in range(1, 4):
        for b in range(2):
            to_hop(r, b).wait_send()
    for d in range(2, 16):
        to_mine(d // 4, d // 2 % 2, d % 2).wait_send()

    def drain(n, carry):
        for i in range(2):
            sib_copy(n, i).wait_send()
        for r in (1, 2, 3):
            rs_copy(n, r).wait_send()
        for way in (1, 3):
            ag_copy(n, way).wait_send()
        ag_second(n).wait_send()
        here, _, remote_copy = act_copies(n)
        pl.when(jnp.logical_not(here))(remote_copy.wait_send)
        return carry

    lax.fori_loop(0, CHUNKS, drain, 0)


def place_kernel(act_in, grad_in, act_out, grad_out, act_buf, grad_buf, in_sem, out_sem):
    parts = [(act_in.at[pl.ds(i * 4, 4)], act_buf.at[pl.ds(i * 4, 4)], act_out.at[pl.ds(i * 4, 4)]) for i in range(2)]
    parts += [(grad_in.at[rows], grad_buf.at[rows], grad_out.at[rows])
              for rows in (pl.ds(i * 256, 256) for i in range(8))]
    loads = [pltpu.make_async_copy(src, buf, in_sem.at[i]) for i, (src, buf, _) in enumerate(parts)]
    stores = [pltpu.make_async_copy(buf, dst, out_sem.at[i]) for i, (_, buf, dst) in enumerate(parts)]
    for load in loads:
        load.start()
    for load, store in zip(loads, stores):
        load.wait()
        store.start()
    for store in stores:
        store.wait()


def local(tokens, weight_up, cotangent):
    dma = pltpu.SemaphoreType.DMA
    bf16, f32 = jnp.bfloat16, jnp.float32
    act, grad = pl.pallas_call(
        kernel,
        name="mlp_up",
        out_shape=(jax.ShapeDtypeStruct((8, ROWS, 2 * COLS), bf16), jax.ShapeDtypeStruct((DEPTH, COLS), f32)),
        in_specs=[pl.BlockSpec(memory_space=pl.ANY)] * 3,
        out_specs=(pl.BlockSpec(memory_space=pltpu.VMEM),) * 2,
        scratch_shapes=[
            pltpu.VMEM((CHUNKS, 2, 2, ROWS, DEPTH), bf16),
            pltpu.VMEM((DEPTH, COLS), bf16),
            pltpu.VMEM((8, ROWS, 2 * COLS), bf16),
            pltpu.VMEM((4, 2, ROWS, 2 * COLS), bf16),
            pltpu.VMEM((8, 2, ROWS, COLS), bf16),
            pltpu.VMEM((CHUNKS, 2, 2, ROWS, COLS), f32),
            pltpu.VMEM((CHUNKS, 2, 2, ROWS, COLS), bf16),
            pltpu.VMEM((CHUNKS, 3, ROWS, COLS), bf16),
            pltpu.VMEM((CHUNKS, 2, 2, ROWS, COLS), bf16),
            pltpu.VMEM((CHUNKS, ROWS, COLS), bf16),
            dma((3,)),
            dma((8,)), dma((8,)),
            dma((4, 8)), dma((4, 8)),
            dma((CHUNKS, 2)), dma((CHUNKS, 2)),
            dma((CHUNKS, 3)), dma((CHUNKS, 3)),
            dma((CHUNKS, 3)), dma((CHUNKS, 3)),
            dma((4, 2)), dma((4, 2)),
            dma((8, 2)), dma((8, 2)),
            dma((CHUNKS,)), dma((8, 2)),
        ],
        compiler_params=pltpu.CompilerParams(
            collective_id=0, has_side_effects=True, vmem_limit_bytes=56 << 20),
    )(tokens.reshape(ROWS, DEPTH), weight_up, cotangent.reshape(8, ROWS, 2 * COLS))
    act, grad = pl.pallas_call(
        place_kernel,
        name="place",
        out_shape=(jax.ShapeDtypeStruct((8, ROWS, 2 * COLS), bf16), jax.ShapeDtypeStruct((DEPTH, COLS), f32)),
        in_specs=[pl.BlockSpec(memory_space=pl.ANY)] * 2,
        out_specs=(pl.BlockSpec(memory_space=pl.ANY),) * 2,
        scratch_shapes=[pltpu.VMEM((8, ROWS, 2 * COLS), bf16), pltpu.VMEM((DEPTH, COLS), f32), dma((10,)), dma((10,))],
        compiler_params=pltpu.CompilerParams(vmem_limit_bytes=56 << 20),
    )(act, grad)
    return act.reshape(1, 8 * ROWS, 2 * COLS), grad


def solution(mesh):
    return jax.shard_map(
        local,
        mesh=mesh,
        in_specs=(P("ja", "ia", "ka"), P("ka", ("ia", "ja")), P("ja", None, ("ia", "ka"))),
        out_specs=(P("ja", None, ("ia", "ka")), P("ka", ("ia", "ja"))),
        check_vma=False,
    )
```

```python
import jax
import jax.numpy as jnp
from jax import lax
from jax.experimental import pallas as pl
from jax.experimental.pallas import tpu as pltpu
from jax.sharding import PartitionSpec as P

MESH = pl.DeviceIdType.MESH
ROWS, DEPTH, COLS = 48, 2048, 384
SPLIT = 256
DIRECT = 12
PAIRS = ((1, 7), (0, 2), (3, 5), (6, 4))
ORDER = (
    (0, 0), (0, 1), (1, 0), (3, 0), (1, 1), (3, 1), (2, 0), (0, 2),
    (0, 3), (2, 1), (1, 2), (3, 2), (2, 2), (1, 3), (3, 3), (2, 3),
)
CHUNKS = len(ORDER)
SLOT = {(dx, dz): (n, i) for n, (dx, p) in enumerate(ORDER) for i, dz in enumerate(PAIRS[p])}
OFF_X = tuple(dx for dx, _ in ORDER)
OFF_Z = tuple(PAIRS[p] for _, p in ORDER)
SCHEDULE = (
    ((("early_out", 0), ("early_x", 1), ("early_x", 3), ("early_out", 1), ("early_out", 3), ("z", 1),
      ("z", 7), ("x_out", 1), ("x_out", 7), ("early_z", 0, 1), ("early_z", 0, 7), ("x", 1, 0),
      ("x", 3, 0), ("sibling", 0, 1), ("sibling", 0, 7), ("sibling", 1, 0), ("sibling", 3, 0), ("early_x", 2),
      ("early_out", 2), ("early_z", 1, 1), ("early_z", 1, 7), ("early_z", 3, 1), ("early_z", 3, 7)), 0, 0, 0),
    ((("near",), ("z", 2), ("z", 6), ("x", 1, 1), ("x", 3, 1), ("x_out", 2),
      ("x_out", 6), ("sibling", 1, 1), ("sibling", 3, 1), ("early_z", 0, 2), ("early_z", 0, 6), ("sibling", 0, 2),
      ("sibling", 0, 6), ("combine", 0), ("early_z", 2, 1), ("early_z", 2, 7), ("early_z", 1, 2), ("early_z", 1, 6),
      ("early_z", 3, 2), ("early_z", 3, 6)), 0, 1, 0),
    ((("x", 1, 7), ("x", 3, 7), ("sibling", 1, 7), ("sibling", 3, 7)), 0, 2, 0),
    ((("x", 2, 0), ("sibling", 2, 0)), 0, 3, 0),
    ((("x", 2, 1), ("sibling", 2, 1), ("combine", 1)), 1, -1, 0),
    ((("combine", 2), ("combine", 3), ("x", 1, 2), ("x", 3, 2), ("sibling", 1, 2), ("sibling", 3, 2)), 2, -1, 0),
    ((("relay", 0), ("z", 3), ("z", 5), ("x_out", 3), ("x_out", 5), ("early_z", 0, 3),
      ("early_z", 0, 5), ("sibling", 0, 3), ("sibling", 0, 5)), 2, 4, 0),
    ((("early_z", 1, 3), ("early_z", 1, 5), ("early_z", 2, 2), ("early_z", 2, 6)), 2, 5, 0),
    ((("x", 1, 6), ("x", 3, 6), ("early_z", 3, 3), ("early_z", 3, 5), ("sibling", 1, 6), ("sibling", 3, 6),
      ("relay", 1)), 4, -1, 1),
    ((("x", 2, 7), ("sibling", 2, 7), ("combine", 4), ("z", 4), ("x_out", 4), ("cot_far",),
      ("early_z", 0, 4), ("sibling", 0, 4), ("early_z", 1, 4), ("combine", 5), ("x", 2, 2), ("sibling", 2, 2),
      ("early_z", 2, 3), ("early_z", 2, 5)), 4, 6, 1),
    ((("early_z", 3, 4), ("relay", 2)), 4, 7, 1),
    ((("relay", 3),), 4, 8, 1),
    ((), 4, 9, 1),
    ((("x", 1, 3), ("x", 3, 3), ("sibling", 1, 3), ("sibling", 3, 3), ("combine", 6)), 6, -1, 1),
    ((("combine", 7),), 6, -1, 2),
    ((("combine", 8),), 6, -1, 3),
    ((("x", 1, 5), ("x", 3, 5), ("sibling", 1, 5), ("sibling", 3, 5), ("combine", 9), ("early_z", 2, 4)), 7, -1, 3),
    ((("x", 2, 6), ("sibling", 2, 6)), 7, -1, 4),
    ((("relay", 4), ("relay", 5)), 7, 10, 4),
    ((), 7, 11, 4),
    ((("relay", 6),), 8, -1, 4),
    ((("x", 1, 4), ("x", 3, 4), ("sibling", 1, 4), ("sibling", 3, 4)), 10, -1, 5),
    ((("x", 2, 3), ("sibling", 2, 3), ("combine", 10)), 10, -1, 6),
    ((("x", 2, 5), ("sibling", 2, 5), ("combine", 11), ("relay", 7)), 10, -1, 7),
    ((), 10, 12, 7),
    ((("x", 2, 4), ("sibling", 2, 4), ("relay", 8), ("relay", 9)), 10, 13, 7),
    ((), 10, 14, 7),
    ((), 10, 15, 7),
    ((("combine", 12),), 12, -1, 8),
    ((("combine", 13), ("combine", 14)), 12, -1, 9),
    ((("combine", 15),), 12, -1, 10),
    ((("relay", 10),), 13, -1, 10),
    ((("relay", 11),), 16, -1, 16),
)


def pick(index, table):
    if isinstance(index, int):
        return table[index]
    out = jnp.int32(table[0])
    for j, entry in enumerate(table[1:], 1):
        out = jnp.where(index == j, jnp.int32(entry), out)
    return out


def mod(value, n):
    return lax.rem(value + 16 * n, n)


def kernel(tok_ref, w_ref, cot_ref, act_ref, grad_ref, xs, ws, cots, hop, mine, pf, pb, terms, slopes, acts,
           load_sem, z_send, z_recv, x_send, x_recv, ez_send, ez_recv, ex_send, ex_recv, sib_send, sib_recv, rs_send, rs_recv, ag_send, ag_recv,
           hop_send, hop_recv, mine_send, mine_recv, act_send, act_recv):
    ia, ja, y = lax.axis_index("ia"), lax.axis_index("ja"), lax.axis_index("ka")
    x, z_lo, z_hi, c = ia // 2, lax.rem(ia, 2), ja // 2, lax.rem(ja, 2)
    z = z_hi * 2 + z_lo

    def device(dx=0, dz=0, dy=0):
        tz = mod(z + dz, 8)
        return (mod(x + dx, 4) * 2 + lax.rem(tz, 2), (tz // 2) * 2 + c, mod(y + dy, 4))

    sibling = (ia, z_hi * 2 + 1 - c, y)

    def remote(src, dst, send, recv, to):
        return pltpu.make_async_remote_copy(
            src_ref=src, dst_ref=dst, send_sem=send, recv_sem=recv, device_id=to, device_id_type=MESH)

    loads = [
        pltpu.make_async_copy(tok_ref, xs.at[SLOT[0, 0][0], SLOT[0, 0][1], 0], load_sem.at[0]),
        pltpu.make_async_copy(cot_ref, cots, load_sem.at[1]),
        pltpu.make_async_copy(w_ref, ws, load_sem.at[2]),
    ]
    for load in loads:
        load.start()

    barrier = pltpu.get_barrier_semaphore()
    for to in [device(dx=1), device(dx=-1), device(dz=1), device(dz=-1)] + [device(dy=r) for r in (1, 2, 3)] + [
            (ia, mod(ja + d, 8), y) for d in range(1, 8)]:
        pl.semaphore_signal(barrier, inc=1, device_id=to, device_id_type=MESH)
    at_home = y == z_hi
    for owner in range(4):
        for core in range(2):
            @pl.when(jnp.logical_not(at_home & (owner == y) & (core == c)))
            def _():
                pl.semaphore_signal(barrier, inc=1, device_id=(ia, y * 2 + core, owner), device_id_type=MESH)
    pl.semaphore_wait(barrier, 14 + 8 - jnp.where(at_home, 1, 0))

    def block(dx, dz, core=0):
        n, i = SLOT[dx, dz]
        return xs.at[n, i, core]

    def early(ref, h=None):
        return ref.at[:, pl.ds(0, SPLIT)] if h is None else ref.at[:, pl.ds(h * (SPLIT // 2), SPLIT // 2)]

    def late(ref, h=None):
        size = (DEPTH - SPLIT) // 2
        return ref.at[:, pl.ds(SPLIT, 2 * size)] if h is None else ref.at[:, pl.ds(SPLIT + h * size, size)]

    def along_z(part, dx, dz, way, sends, recvs):
        to, h = (dz + way) % 8, (None if (dz + way) % 8 != 4 else (0 if way == 1 else 1))
        at = to if h is None else 4 * h
        return remote(part(block(dx, dz), h), part(block(dx, to), h), sends.at[dx, at], recvs.at[dx, at], device(dz=way))

    def along_x(part, dz, dx, way, sends, recvs):
        to, h = (dx + way) % 4, (None if (dx + way) % 4 != 2 else (0 if way == 1 else 1))
        at = to if h is None else 2 * h
        return remote(part(block(dx, dz), h), part(block(to, dz), h), sends.at[at, dz], recvs.at[at, dz], device(dx=way))

    def z_late(dz, way):
        return along_z(late, 0, dz, way, z_send, z_recv)

    def x_late(dz, dx, way):
        return along_x(late, dz, dx, way, x_send, x_recv)

    def x_early(dx, way):
        return along_x(early, 0, dx, way, ex_send, ex_recv)

    def z_early(dx, dz, way):
        return along_z(early, dx, dz, way, ez_send, ez_recv)

    def sib_copy(n, i):
        return remote(xs.at[n, i, 0], xs.at[n, i, 1], sib_send.at[n, i], sib_recv.at[n, i], sibling)

    def to_sibling(dx, dz):
        sib_copy(*SLOT[dx, dz]).start()

    def ring_step(copy, at, size):
        if at == size // 2:
            copy(at - 1, 1).wait_recv()
            copy(at + 1, -1).wait_recv()
        else:
            way = 1 if at < size // 2 else -1
            copy((at - way) % size, way).wait_recv()
            copy(at, way).start()

    def z_arrive(dz):
        ring_step(z_late, dz, 8)

    def x_out(*dzs):
        for dz in dzs:
            x_late(dz, 0, 1).start()
            x_late(dz, 0, -1).start()

    def x_arrive(dx, dz):
        ring_step(lambda at, way: x_late(dz, at, way), dx, 4)

    def early_x(dx):
        ring_step(x_early, dx, 4)

    def early_out(dx):
        z_early(dx, 0, 1).start()
        z_early(dx, 0, -1).start()

    def early_z(dx, dz):
        ring_step(lambda at, way: z_early(dx, at, way), dz, 8)

    def to_mine(dz, other, b):
        tz, tc = mod(z_hi + dz, 4), (1 - c if other else c)
        src = hop.at[mod(y - tz, 4), b, :, pl.ds(pl.multiple_of(tc * COLS, COLS), COLS)]
        d = dz * 2 + other
        if d == 0:
            return pltpu.make_async_copy(src, mine.at[0, b], mine_recv.at[0, b])
        return remote(src, mine.at[d, b], mine_send.at[d, b], mine_recv.at[d, b], (ia, tz * 2 + tc, y))

    def to_hop(r, b):
        at = mod(y + r - z_hi * 2 - b - c, 4) * 2 + b
        if r == 0:
            return pltpu.make_async_copy(cots.at[at], hop.at[0, b], hop_recv.at[0, b])
        return remote(cots.at[at], hop.at[r, b], hop_send.at[r, b], hop_recv.at[r, b], device(dy=r))

    def cot_near():
        for r in range(4):
            for b in range(2):
                to_hop(r, b).wait_recv() if r else to_hop(r, b).wait()
        for dz in (0, 1, 3):
            for other in (0, 1):
                for b in range(2):
                    to_mine(dz, other, b).start()

    def cot_far():
        for other in (0, 1):
            for b in range(2):
                to_mine(2, other, b).start()

    loads[0].wait()
    for way in (1, -1):
        z_late(0, way).start()
    for way in (1, -1):
        x_early(0, way).start()
    x_out(0)
    to_sibling(0, 0)
    loads[1].wait()
    for r in range(4):
        for b in range(2):
            to_hop(r, b).start()
    grad_ref[...] = jnp.zeros_like(grad_ref)
    loads[2].wait()

    def place(n, r):
        first = pick(n, [pair[0] for pair in OFF_Z])
        v = mod(y + r - x + pick(n, OFF_X) - z + first, 4)
        i = v // 2
        return i, lax.rem(v + c, 2)

    def way_of(n):
        return 1 + 2 * (n % 2)

    def rs_far(n):
        i, k = place(n, 2)
        return remote(pb.at[n, i, k], terms.at[n, 2], rs_send.at[n, 2], rs_recv.at[n, 2], device(dy=way_of(n)))

    def rs_sum(n):
        i, k = place(n, way_of(n))
        return remote(pb.at[n, i, k], terms.at[n, 0], rs_send.at[n, 0], rs_recv.at[n, 0], device(dy=way_of(n)))

    def rs_near(n):
        i, k = place(n, 4 - way_of(n))
        return remote(pb.at[n, i, k], terms.at[n, 1], rs_send.at[n, 1], rs_recv.at[n, 1], device(dy=4 - way_of(n)))

    def combine(n):
        rs_far(n).wait_recv()
        i, k = place(n, way_of(n))
        pb[n, i, k] = (pf[n, i, k] + terms[n, 2].astype(jnp.float32)).astype(jnp.bfloat16)
        rs_sum(n).start()

    def ag_copy(n, way):
        i, k = place(n, 0)
        return remote(slopes.at[n, i, k], slopes.at[n, i, k], ag_send.at[n, way - 1], ag_recv.at[n, way - 1],
                      device(dy=way))

    def ag_second(n):
        way = way_of(n)
        i, k = place(n, 4 - way)
        return remote(slopes.at[n, i, k], slopes.at[n, i, k], ag_send.at[n, 1], ag_recv.at[n, 1], device(dy=way))

    def ag_direct(n):
        i, k = place(n, 0)
        return remote(slopes.at[n, i, k], slopes.at[n, i, k], ag_send.at[n, 1], ag_recv.at[n, 1], device(dy=2))

    def relay(n):
        ag_copy(n, 1 + 2 * (n % 2)).wait_recv()
        ag_second(n).start()

    def source(n):
        i, k = place(n, 0)
        dz = jnp.where(i == 0, pick(n, [pair[0] for pair in OFF_Z]), pick(n, [pair[1] for pair in OFF_Z]))
        return mod(x - pick(n, OFF_X), 4), mod(z - dz, 8), lax.rem(c + k, 2)

    def act_copies(n):
        sx, sz, sc = source(n)
        at = sx * 2 + lax.rem(sz, 2)
        dst = act_ref.at[at, :, pl.ds(pl.multiple_of(c * COLS, COLS), COLS)]
        here = at_home & (sz // 2 == z_hi) & (sc == c)
        to = (ia, (sz // 2) * 2 + sc, z_hi)
        return (here, pltpu.make_async_copy(acts.at[n], dst, act_recv.at[at, c]),
                remote(acts.at[n], dst, act_send.at[n], act_recv.at[at, c], to))

    def forward(n):
        for i in range(2):
            sib_copy(n, i).wait_recv()
        out = jnp.dot(xs[n].reshape(4 * ROWS, DEPTH), ws[...], preferred_element_type=jnp.float32)
        pf[n] = out.reshape(2, 2, ROWS, COLS)
        pb[n] = out.astype(jnp.bfloat16).reshape(2, 2, ROWS, COLS)
        rs_far(n).start()
        rs_near(n).start()

    def middle(n):
        rs_near(n).wait_recv()
        rs_sum(n).wait_recv()
        i, k = place(n, 0)
        _, sz, sc = source(n)
        pre = pf[n, i, k] + terms[n, 0].astype(jnp.float32) + terms[n, 1].astype(jnp.float32)
        d, b = mod(z_hi - sz // 2, 4) * 2 + lax.rem(sc + c, 2), lax.rem(sz, 2)
        pltpu.make_async_copy(mine.at[d, b], mine.at[d, b], mine_recv.at[d, b]).wait()
        cot = mine[d, b].astype(jnp.float32)
        root = 0.7978845608028654
        square = pre * pre
        t = jnp.tanh(root * pre * (1.0 + 0.044715 * square))
        slope = 0.5 * (1.0 + t) + 0.5 * pre * (1.0 - t * t) * (root * (1.0 + 3 * 0.044715 * square))
        slopes[n, i, k] = (cot * slope).astype(jnp.bfloat16)
        for r in (1, 3):
            ag_copy(n, r).start()
        if n >= DIRECT:
            ag_direct(n).start()
        acts[n] = (0.5 * pre * (1.0 + t)).astype(jnp.bfloat16)
        here, local_copy, remote_copy = act_copies(n)
        pl.when(here)(local_copy.start)
        pl.when(jnp.logical_not(here))(remote_copy.start)

    def backward(n):
        ag_copy(n, 3 - 2 * (n % 2)).wait_recv()
        ag_second(n).wait_recv()
        if n >= DIRECT:
            ag_copy(n, 1 + 2 * (n % 2)).wait_recv()
        s = slopes[n].reshape(4 * ROWS, COLS)
        for b in range(4):
            cols = pl.ds(b * 512, 512)
            grad_ref[cols, :] += lax.dot_general(
                xs[n, :, :, :, cols].reshape(4 * ROWS, 512), s, (((0,), (0,)), ((), ())),
                preferred_element_type=jnp.float32)

    actions = {
        "z": z_arrive, "x_out": x_out, "x": x_arrive, "early_x": early_x, "early_out": early_out, "early_z": early_z,
        "sibling": to_sibling,
        "near": cot_near, "cot_far": cot_far, "relay": relay, "combine": combine,
    }
    mids, grads = [0], [0]
    for _, mid, _, grad in SCHEDULE:
        mids.append(mid)
        grads.append(grad)

    for t, (events, _, chunk, _) in enumerate(SCHEDULE):
        for name, *args in events:
            actions[name](*args)
        for n in range(mids[t], mids[t + 1]):
            middle(n)
        if chunk >= 0:
            forward(chunk)
        for n in range(grads[t], grads[t + 1]):
            backward(n)

    for at in range(8):
        for core in range(2):
            dst = act_ref.at[at, :, pl.ds(core * COLS, COLS)]
            pltpu.make_async_copy(acts.at[0], dst, act_recv.at[at, core]).wait()
    for dz in (0, 1, 2, 3, 7, 6, 5):
        for way in ((1, -1) if dz == 0 else (1,) if dz < 4 else (-1,)):
            z_late(dz, way).wait_send()
            for dx in range(4):
                z_early(dx, dz, way).wait_send()
    for dx, way in ((0, 1), (0, -1), (1, 1), (3, -1)):
        x_early(dx, way).wait_send()
        for dz in range(8):
            x_late(dz, dx, way).wait_send()
    for r in range(1, 4):
        for b in range(2):
            to_hop(r, b).wait_send()
    for d in range(2, 16):
        to_mine(d // 4, d // 2 % 2, d % 2).wait_send()

    def drain(n, carry):
        for i in range(2):
            sib_copy(n, i).wait_send()
        for copy in (rs_far(n), rs_near(n), rs_sum(n)):
            copy.wait_send()
        for way in (1, 3):
            ag_copy(n, way).wait_send()
        ag_second(n).wait_send()
        here, _, remote_copy = act_copies(n)
        pl.when(jnp.logical_not(here))(remote_copy.wait_send)
        return carry

    lax.fori_loop(0, CHUNKS, drain, 0)


def place_kernel(act_in, grad_in, act_out, grad_out, sem):
    copies = [pltpu.make_async_copy(act_in, act_out, sem.at[0]), pltpu.make_async_copy(grad_in, grad_out, sem.at[1])]
    for copy in copies:
        copy.start()
    for copy in copies:
        copy.wait()


def local(tokens, weight_up, cotangent):
    dma = pltpu.SemaphoreType.DMA
    bf16, f32 = jnp.bfloat16, jnp.float32
    act, grad = pl.pallas_call(
        kernel,
        name="mlp_up",
        out_shape=(pltpu.VMEM((8, ROWS, 2 * COLS), bf16), pltpu.VMEM((DEPTH, COLS), f32)),
        in_specs=[pl.BlockSpec(memory_space=pl.ANY)] * 3,
        out_specs=(pl.BlockSpec(memory_space=pltpu.VMEM),) * 2,
        scratch_shapes=[
            pltpu.VMEM((CHUNKS, 2, 2, ROWS, DEPTH), bf16),
            pltpu.VMEM((DEPTH, COLS), bf16),
            pltpu.VMEM((8, ROWS, 2 * COLS), bf16),
            pltpu.VMEM((4, 2, ROWS, 2 * COLS), bf16),
            pltpu.VMEM((8, 2, ROWS, COLS), bf16),
            pltpu.VMEM((CHUNKS, 2, 2, ROWS, COLS), f32),
            pltpu.VMEM((CHUNKS, 2, 2, ROWS, COLS), bf16),
            pltpu.VMEM((CHUNKS, 3, ROWS, COLS), bf16),
            pltpu.VMEM((CHUNKS, 2, 2, ROWS, COLS), bf16),
            pltpu.VMEM((CHUNKS, ROWS, COLS), bf16),
            dma((3,)),
            dma((1, 8)), dma((1, 8)),
            dma((4, 8)), dma((4, 8)),
            dma((4, 8)), dma((4, 8)),
            dma((4, 1)), dma((4, 1)),
            dma((CHUNKS, 2)), dma((CHUNKS, 2)),
            dma((CHUNKS, 3)), dma((CHUNKS, 3)),
            dma((CHUNKS, 3)), dma((CHUNKS, 3)),
            dma((4, 2)), dma((4, 2)),
            dma((8, 2)), dma((8, 2)),
            dma((CHUNKS,)), dma((8, 2)),
        ],
        compiler_params=pltpu.CompilerParams(
            collective_id=0, has_side_effects=True, vmem_limit_bytes=56 << 20),
    )(tokens.reshape(ROWS, DEPTH), weight_up, cotangent.reshape(8, ROWS, 2 * COLS))
    act, grad = pl.pallas_call(
        place_kernel,
        name="place",
        out_shape=(jax.ShapeDtypeStruct((8, ROWS, 2 * COLS), bf16), jax.ShapeDtypeStruct((DEPTH, COLS), f32)),
        in_specs=[pl.BlockSpec(memory_space=pltpu.VMEM)] * 2,
        out_specs=(pl.BlockSpec(memory_space=pl.ANY),) * 2,
        scratch_shapes=[dma((2,))],
        compiler_params=pltpu.CompilerParams(vmem_limit_bytes=56 << 20),
    )(pltpu.with_memory_space_constraint(act, pltpu.VMEM), pltpu.with_memory_space_constraint(grad, pltpu.VMEM))
    return act.reshape(1, 8 * ROWS, 2 * COLS), grad


def solution(mesh):
    return jax.shard_map(
        local,
        mesh=mesh,
        in_specs=(P("ja", "ia", "ka"), P("ka", ("ia", "ja")), P("ja", None, ("ia", "ka"))),
        out_specs=(P("ja", None, ("ia", "ka")), P("ka", ("ia", "ja"))),
        check_vma=False,
    )
```

```python
import jax
import jax.numpy as jnp
from jax import lax
from jax.experimental import pallas as pl
from jax.experimental.pallas import tpu as pltpu
from jax.sharding import PartitionSpec as P

MESH = pl.DeviceIdType.MESH
ROWS, DEPTH, COLS = 48, 2048, 384
SPLIT = 256
DIRECT = 12
PAIRS = ((1, 7), (0, 2), (3, 5), (6, 4))
ORDER = (
    (0, 0), (0, 1), (1, 0), (3, 0), (1, 1), (3, 1), (2, 0), (0, 2),
    (0, 3), (2, 1), (1, 2), (3, 2), (2, 2), (1, 3), (3, 3), (2, 3),
)
CHUNKS = len(ORDER)
SLOT = {(dx, dz): (n, i) for n, (dx, p) in enumerate(ORDER) for i, dz in enumerate(PAIRS[p])}
OFF_X = tuple(dx for dx, _ in ORDER)
OFF_Z = tuple(PAIRS[p] for _, p in ORDER)
SCHEDULE = (
    ((("early_out", 0), ("early_x", 1), ("early_x", 3), ("early_out", 1), ("early_out", 3), ("z", 1),
      ("z", 7), ("x_out", 1), ("x_out", 7), ("early_z", 0, 1), ("early_z", 0, 7), ("x", 1, 0),
      ("x", 3, 0), ("sibling", 0, 1), ("sibling", 0, 7), ("sibling", 1, 0), ("sibling", 3, 0), ("early_x", 2),
      ("early_out", 2), ("early_z", 1, 1), ("early_z", 1, 7), ("early_z", 3, 1), ("early_z", 3, 7)), 0, 0, 0),
    ((("near",), ("z", 2), ("z", 6), ("x", 1, 1), ("x", 3, 1), ("x_out", 2),
      ("x_out", 6), ("sibling", 1, 1), ("sibling", 3, 1), ("early_z", 0, 2), ("early_z", 0, 6), ("sibling", 0, 2),
      ("sibling", 0, 6), ("combine", 0), ("early_z", 2, 1), ("early_z", 2, 7), ("early_z", 1, 2), ("early_z", 1, 6),
      ("early_z", 3, 2), ("early_z", 3, 6)), 0, 1, 0),
    ((("x", 1, 7), ("x", 3, 7), ("sibling", 1, 7), ("sibling", 3, 7)), 0, 2, 0),
    ((("x", 2, 0), ("sibling", 2, 0)), 0, 3, 0),
    ((("x", 2, 1), ("sibling", 2, 1), ("combine", 1)), 1, -1, 0),
    ((("combine", 2), ("combine", 3), ("x", 1, 2), ("x", 3, 2), ("sibling", 1, 2), ("sibling", 3, 2)), 2, -1, 0),
    ((("relay", 0), ("z", 3), ("z", 5), ("x_out", 3), ("x_out", 5), ("early_z", 0, 3),
      ("early_z", 0, 5), ("sibling", 0, 3), ("sibling", 0, 5)), 2, 4, 0),
    ((("early_z", 1, 3), ("early_z", 1, 5), ("early_z", 2, 2), ("early_z", 2, 6)), 2, 5, 0),
    ((("x", 1, 6), ("x", 3, 6), ("early_z", 3, 3), ("early_z", 3, 5), ("sibling", 1, 6), ("sibling", 3, 6),
      ("relay", 1)), 4, -1, 1),
    ((("x", 2, 7), ("sibling", 2, 7), ("combine", 4), ("z", 4), ("x_out", 4), ("cot_far",),
      ("early_z", 0, 4), ("sibling", 0, 4), ("early_z", 1, 4), ("combine", 5), ("x", 2, 2), ("sibling", 2, 2),
      ("early_z", 2, 3), ("early_z", 2, 5)), 4, 6, 1),
    ((("early_z", 3, 4), ("relay", 2)), 4, 7, 1),
    ((("relay", 3),), 4, 8, 1),
    ((), 4, 9, 1),
    ((("x", 1, 3), ("x", 3, 3), ("sibling", 1, 3), ("sibling", 3, 3), ("combine", 6)), 6, -1, 1),
    ((("combine", 7),), 6, -1, 2),
    ((("combine", 8),), 6, -1, 3),
    ((("x", 1, 5), ("x", 3, 5), ("sibling", 1, 5), ("sibling", 3, 5), ("combine", 9), ("early_z", 2, 4)), 7, -1, 3),
    ((("x", 2, 6), ("sibling", 2, 6)), 7, -1, 4),
    ((("relay", 4), ("relay", 5)), 7, 10, 4),
    ((), 7, 11, 4),
    ((("relay", 6),), 8, -1, 4),
    ((("x", 1, 4), ("x", 3, 4), ("sibling", 1, 4), ("sibling", 3, 4)), 10, -1, 5),
    ((("x", 2, 3), ("sibling", 2, 3), ("combine", 10)), 10, -1, 6),
    ((("x", 2, 5), ("sibling", 2, 5), ("combine", 11), ("relay", 7)), 10, -1, 7),
    ((), 10, 12, 7),
    ((("x", 2, 4), ("sibling", 2, 4), ("relay", 8), ("relay", 9)), 10, 13, 7),
    ((), 10, 14, 7),
    ((), 10, 15, 7),
    ((("combine", 12),), 12, -1, 8),
    ((("combine", 13), ("combine", 14)), 12, -1, 9),
    ((("combine", 15),), 12, -1, 10),
    ((("relay", 10),), 13, -1, 10),
    ((("relay", 11),), 16, -1, 16),
)


def pick(index, table):
    if isinstance(index, int):
        return table[index]
    out = jnp.int32(table[0])
    for j, entry in enumerate(table[1:], 1):
        out = jnp.where(index == j, jnp.int32(entry), out)
    return out


def mod(value, n):
    return lax.rem(value + 16 * n, n)


def kernel(tok_ref, w_ref, cot_ref, act_ref, grad_ref, xs, ws, cots, hop, mine, pf, pb, terms, slopes, acts,
           load_sem, z_send, z_recv, x_send, x_recv, ez_send, ez_recv, ex_send, ex_recv, sib_send, sib_recv, rs_send, rs_recv, ag_send, ag_recv,
           hop_send, hop_recv, mine_send, mine_recv, act_send, act_recv):
    ia, ja, y = lax.axis_index("ia"), lax.axis_index("ja"), lax.axis_index("ka")
    x, z_lo, z_hi, c = ia // 2, lax.rem(ia, 2), ja // 2, lax.rem(ja, 2)
    z = z_hi * 2 + z_lo

    def device(dx=0, dz=0, dy=0):
        tz = mod(z + dz, 8)
        return (mod(x + dx, 4) * 2 + lax.rem(tz, 2), (tz // 2) * 2 + c, mod(y + dy, 4))

    sibling = (ia, z_hi * 2 + 1 - c, y)

    def remote(src, dst, send, recv, to):
        return pltpu.make_async_remote_copy(
            src_ref=src, dst_ref=dst, send_sem=send, recv_sem=recv, device_id=to, device_id_type=MESH)

    barrier = pltpu.get_barrier_semaphore()
    at_home = y == z_hi
    for owner in range(4):
        for core in range(2):
            @pl.when(jnp.logical_not(at_home & (owner == y) & (core == c)))
            def _():
                pl.semaphore_signal(barrier, inc=1, device_id=(ia, y * 2 + core, owner), device_id_type=MESH)
    for to in [(ia, mod(ja + d, 8), y) for d in (4, 5, 3, 2, 6, 7, 1)] + [device(dy=r) for r in (2, 1, 3)] + [
            device(dz=1), device(dz=-1), device(dx=1), device(dx=-1)]:
        pl.semaphore_signal(barrier, inc=1, device_id=to, device_id_type=MESH)
    loads = [
        pltpu.make_async_copy(tok_ref, xs.at[SLOT[0, 0][0], SLOT[0, 0][1], 0], load_sem.at[0]),
        pltpu.make_async_copy(cot_ref, cots, load_sem.at[1]),
        pltpu.make_async_copy(w_ref, ws, load_sem.at[2]),
    ]
    for load in loads:
        load.start()
    pl.semaphore_wait(barrier, 14 + 8 - jnp.where(at_home, 1, 0))

    def block(dx, dz, core=0):
        n, i = SLOT[dx, dz]
        return xs.at[n, i, core]

    def early(ref, h=None):
        return ref.at[:, pl.ds(0, SPLIT)] if h is None else ref.at[:, pl.ds(h * (SPLIT // 2), SPLIT // 2)]

    def late(ref, h=None):
        size = (DEPTH - SPLIT) // 2
        return ref.at[:, pl.ds(SPLIT, 2 * size)] if h is None else ref.at[:, pl.ds(SPLIT + h * size, size)]

    def along_z(part, dx, dz, way, sends, recvs):
        to, h = (dz + way) % 8, (None if (dz + way) % 8 != 4 else (0 if way == 1 else 1))
        at = to if h is None else 4 * h
        return remote(part(block(dx, dz), h), part(block(dx, to), h), sends.at[dx, at], recvs.at[dx, at], device(dz=way))

    def along_x(part, dz, dx, way, sends, recvs):
        to, h = (dx + way) % 4, (None if (dx + way) % 4 != 2 else (0 if way == 1 else 1))
        at = to if h is None else 2 * h
        return remote(part(block(dx, dz), h), part(block(to, dz), h), sends.at[at, dz], recvs.at[at, dz], device(dx=way))

    def z_late(dz, way):
        return along_z(late, 0, dz, way, z_send, z_recv)

    def x_late(dz, dx, way):
        return along_x(late, dz, dx, way, x_send, x_recv)

    def x_early(dx, way):
        return along_x(early, 0, dx, way, ex_send, ex_recv)

    def z_early(dx, dz, way):
        return along_z(early, dx, dz, way, ez_send, ez_recv)

    def sib_copy(n, i):
        return remote(xs.at[n, i, 0], xs.at[n, i, 1], sib_send.at[n, i], sib_recv.at[n, i], sibling)

    def to_sibling(dx, dz):
        sib_copy(*SLOT[dx, dz]).start()

    def ring_step(copy, at, size):
        if at == size // 2:
            copy(at - 1, 1).wait_recv()
            copy(at + 1, -1).wait_recv()
        else:
            way = 1 if at < size // 2 else -1
            copy((at - way) % size, way).wait_recv()
            copy(at, way).start()

    def z_arrive(dz):
        ring_step(z_late, dz, 8)

    def x_out(*dzs):
        for dz in dzs:
            x_late(dz, 0, 1).start()
            x_late(dz, 0, -1).start()

    def x_arrive(dx, dz):
        ring_step(lambda at, way: x_late(dz, at, way), dx, 4)

    def early_x(dx):
        ring_step(x_early, dx, 4)

    def early_out(dx):
        z_early(dx, 0, 1).start()
        z_early(dx, 0, -1).start()

    def early_z(dx, dz):
        ring_step(lambda at, way: z_early(dx, at, way), dz, 8)

    def to_mine(dz, other, b):
        tz, tc = mod(z_hi + dz, 4), (1 - c if other else c)
        src = hop.at[mod(y - tz, 4), b, :, pl.ds(pl.multiple_of(tc * COLS, COLS), COLS)]
        d = dz * 2 + other
        if d == 0:
            return pltpu.make_async_copy(src, mine.at[0, b], mine_recv.at[0, b])
        return remote(src, mine.at[d, b], mine_send.at[d, b], mine_recv.at[d, b], (ia, tz * 2 + tc, y))

    def to_hop(r, b):
        at = mod(y + r - z_hi * 2 - b - c, 4) * 2 + b
        if r == 0:
            return pltpu.make_async_copy(cots.at[at], hop.at[0, b], hop_recv.at[0, b])
        return remote(cots.at[at], hop.at[r, b], hop_send.at[r, b], hop_recv.at[r, b], device(dy=r))

    def cot_near():
        for r in range(4):
            for b in range(2):
                to_hop(r, b).wait_recv() if r else to_hop(r, b).wait()
        for dz in (0, 1, 3):
            for other in (0, 1):
                for b in range(2):
                    to_mine(dz, other, b).start()

    def cot_far():
        for other in (0, 1):
            for b in range(2):
                to_mine(2, other, b).start()

    loads[0].wait()
    for way in (1, -1):
        z_late(0, way).start()
    for way in (1, -1):
        x_early(0, way).start()
    x_out(0)
    to_sibling(0, 0)
    loads[1].wait()
    for r in range(4):
        for b in range(2):
            to_hop(r, b).start()
    grad_ref[...] = jnp.zeros_like(grad_ref)
    loads[2].wait()

    def place(n, r):
        first = pick(n, [pair[0] for pair in OFF_Z])
        v = mod(y + r - x + pick(n, OFF_X) - z + first, 4)
        i = v // 2
        return i, lax.rem(v + c, 2)

    def way_of(n):
        return 1 + 2 * (n % 2)

    def rs_far(n):
        i, k = place(n, 2)
        return remote(pb.at[n, i, k], terms.at[n, 2], rs_send.at[n, 2], rs_recv.at[n, 2], device(dy=way_of(n)))

    def rs_sum(n):
        i, k = place(n, way_of(n))
        return remote(pb.at[n, i, k], terms.at[n, 0], rs_send.at[n, 0], rs_recv.at[n, 0], device(dy=way_of(n)))

    def rs_near(n):
        i, k = place(n, 4 - way_of(n))
        return remote(pb.at[n, i, k], terms.at[n, 1], rs_send.at[n, 1], rs_recv.at[n, 1], device(dy=4 - way_of(n)))

    def combine(n):
        rs_far(n).wait_recv()
        i, k = place(n, way_of(n))
        pb[n, i, k] = (pf[n, i, k] + terms[n, 2].astype(jnp.float32)).astype(jnp.bfloat16)
        rs_sum(n).start()

    def ag_copy(n, way):
        i, k = place(n, 0)
        return remote(slopes.at[n, i, k], slopes.at[n, i, k], ag_send.at[n, way - 1], ag_recv.at[n, way - 1],
                      device(dy=way))

    def ag_second(n):
        way = way_of(n)
        i, k = place(n, 4 - way)
        return remote(slopes.at[n, i, k], slopes.at[n, i, k], ag_send.at[n, 1], ag_recv.at[n, 1], device(dy=way))

    def ag_direct(n):
        i, k = place(n, 0)
        return remote(slopes.at[n, i, k], slopes.at[n, i, k], ag_send.at[n, 1], ag_recv.at[n, 1], device(dy=2))

    def relay(n):
        ag_copy(n, 1 + 2 * (n % 2)).wait_recv()
        ag_second(n).start()

    def source(n):
        i, k = place(n, 0)
        dz = jnp.where(i == 0, pick(n, [pair[0] for pair in OFF_Z]), pick(n, [pair[1] for pair in OFF_Z]))
        return mod(x - pick(n, OFF_X), 4), mod(z - dz, 8), lax.rem(c + k, 2)

    def act_copies(n):
        sx, sz, sc = source(n)
        at = sx * 2 + lax.rem(sz, 2)
        dst = act_ref.at[at, :, pl.ds(pl.multiple_of(c * COLS, COLS), COLS)]
        here = at_home & (sz // 2 == z_hi) & (sc == c)
        to = (ia, (sz // 2) * 2 + sc, z_hi)
        return (here, pltpu.make_async_copy(acts.at[n], dst, act_recv.at[at, c]),
                remote(acts.at[n], dst, act_send.at[n], act_recv.at[at, c], to))

    def forward(n):
        for i in range(2):
            sib_copy(n, i).wait_recv()
        out = jnp.dot(xs[n].reshape(4 * ROWS, DEPTH), ws[...], preferred_element_type=jnp.float32)
        pf[n] = out.reshape(2, 2, ROWS, COLS)
        pb[n] = out.astype(jnp.bfloat16).reshape(2, 2, ROWS, COLS)
        rs_far(n).start()
        rs_near(n).start()

    def middle(n):
        rs_near(n).wait_recv()
        rs_sum(n).wait_recv()
        i, k = place(n, 0)
        _, sz, sc = source(n)
        pre = pf[n, i, k] + terms[n, 0].astype(jnp.float32) + terms[n, 1].astype(jnp.float32)
        d, b = mod(z_hi - sz // 2, 4) * 2 + lax.rem(sc + c, 2), lax.rem(sz, 2)
        pltpu.make_async_copy(mine.at[d, b], mine.at[d, b], mine_recv.at[d, b]).wait()
        cot = mine[d, b].astype(jnp.float32)
        root = 0.7978845608028654
        square = pre * pre
        t = jnp.tanh(root * pre * (1.0 + 0.044715 * square))
        slope = 0.5 * (1.0 + t) + 0.5 * pre * (1.0 - t * t) * (root * (1.0 + 3 * 0.044715 * square))
        slopes[n, i, k] = (cot * slope).astype(jnp.bfloat16)
        for r in (1, 3):
            ag_copy(n, r).start()
        if n >= DIRECT:
            ag_direct(n).start()
        acts[n] = (0.5 * pre * (1.0 + t)).astype(jnp.bfloat16)
        here, local_copy, remote_copy = act_copies(n)
        pl.when(here)(local_copy.start)
        pl.when(jnp.logical_not(here))(remote_copy.start)

    def backward(n):
        ag_copy(n, 3 - 2 * (n % 2)).wait_recv()
        ag_second(n).wait_recv()
        if n >= DIRECT:
            ag_copy(n, 1 + 2 * (n % 2)).wait_recv()
        s = slopes[n].reshape(4 * ROWS, COLS)
        for b in range(4):
            cols = pl.ds(b * 512, 512)
            grad_ref[cols, :] += lax.dot_general(
                xs[n, :, :, :, cols].reshape(4 * ROWS, 512), s, (((0,), (0,)), ((), ())),
                preferred_element_type=jnp.float32)

    actions = {
        "z": z_arrive, "x_out": x_out, "x": x_arrive, "early_x": early_x, "early_out": early_out, "early_z": early_z,
        "sibling": to_sibling,
        "near": cot_near, "cot_far": cot_far, "relay": relay, "combine": combine,
    }
    mids, grads = [0], [0]
    for _, mid, _, grad in SCHEDULE:
        mids.append(mid)
        grads.append(grad)

    def drain_tokens():
        for dz in (0, 1, 2, 3, 7, 6, 5):
            for way in ((1, -1) if dz == 0 else (1,) if dz < 4 else (-1,)):
                z_late(dz, way).wait_send()
                for dx in range(4):
                    z_early(dx, dz, way).wait_send()
        for dx, way in ((0, 1), (0, -1), (1, 1), (3, -1)):
            x_early(dx, way).wait_send()
            for dz in range(8):
                x_late(dz, dx, way).wait_send()
        for r in range(1, 4):
            for b in range(2):
                to_hop(r, b).wait_send()
        for d in range(2, 16):
            to_mine(d // 4, d // 2 % 2, d % 2).wait_send()

    def drain_chunk(n):
        for copy in (sib_copy(n, 0), sib_copy(n, 1)):
            copy.wait_send()
        for j in range(3):
            remote(pb.at[n, 0, 0], terms.at[n, j], rs_send.at[n, j], rs_recv.at[n, j], sibling).wait_send()
            remote(slopes.at[n, 0, 0], slopes.at[n, 0, 0], ag_send.at[n, j], ag_recv.at[n, j], sibling).wait_send()

    def drain_act(n):
        here, _, remote_copy = act_copies(n)
        pl.when(jnp.logical_not(here))(remote_copy.wait_send)

    for t, (events, _, chunk, _) in enumerate(SCHEDULE):
        for name, *args in events:
            actions[name](*args)
        for n in range(mids[t], mids[t + 1]):
            middle(n)
        if chunk >= 0:
            forward(chunk)
        for n in range(grads[t], grads[t + 1]):
            backward(n)
            if n == 10:
                drain_tokens()
            drain_chunk(n)
            if n >= 2:
                drain_act(n - 2)

    for n in (CHUNKS - 2, CHUNKS - 1):
        drain_act(n)
    for at in range(8):
        for core in range(2):
            dst = act_ref.at[at, :, pl.ds(core * COLS, COLS)]
            pltpu.make_async_copy(acts.at[0], dst, act_recv.at[at, core]).wait()


def place_kernel(act_in, grad_in, act_out, grad_out, sem):
    copies = [pltpu.make_async_copy(act_in, act_out, sem.at[0]), pltpu.make_async_copy(grad_in, grad_out, sem.at[1])]
    for copy in copies:
        copy.start()
    for copy in copies:
        copy.wait()


def local(tokens, weight_up, cotangent):
    dma = pltpu.SemaphoreType.DMA
    bf16, f32 = jnp.bfloat16, jnp.float32
    act, grad = pl.pallas_call(
        kernel,
        name="mlp_up",
        out_shape=(pltpu.VMEM((8, ROWS, 2 * COLS), bf16), pltpu.VMEM((DEPTH, COLS), f32)),
        in_specs=[pl.BlockSpec(memory_space=pl.ANY)] * 3,
        out_specs=(pl.BlockSpec(memory_space=pltpu.VMEM),) * 2,
        scratch_shapes=[
            pltpu.VMEM((CHUNKS, 2, 2, ROWS, DEPTH), bf16),
            pltpu.VMEM((DEPTH, COLS), bf16),
            pltpu.VMEM((8, ROWS, 2 * COLS), bf16),
            pltpu.VMEM((4, 2, ROWS, 2 * COLS), bf16),
            pltpu.VMEM((8, 2, ROWS, COLS), bf16),
            pltpu.VMEM((CHUNKS, 2, 2, ROWS, COLS), f32),
            pltpu.VMEM((CHUNKS, 2, 2, ROWS, COLS), bf16),
            pltpu.VMEM((CHUNKS, 3, ROWS, COLS), bf16),
            pltpu.VMEM((CHUNKS, 2, 2, ROWS, COLS), bf16),
            pltpu.VMEM((CHUNKS, ROWS, COLS), bf16),
            dma((3,)),
            dma((1, 8)), dma((1, 8)),
            dma((4, 8)), dma((4, 8)),
            dma((4, 8)), dma((4, 8)),
            dma((4, 1)), dma((4, 1)),
            dma((CHUNKS, 2)), dma((CHUNKS, 2)),
            dma((CHUNKS, 3)), dma((CHUNKS, 3)),
            dma((CHUNKS, 3)), dma((CHUNKS, 3)),
            dma((4, 2)), dma((4, 2)),
            dma((8, 2)), dma((8, 2)),
            dma((CHUNKS,)), dma((8, 2)),
        ],
        compiler_params=pltpu.CompilerParams(
            collective_id=0, has_side_effects=True, vmem_limit_bytes=56 << 20),
    )(tokens.reshape(ROWS, DEPTH), weight_up, cotangent.reshape(8, ROWS, 2 * COLS))
    act, grad = pl.pallas_call(
        place_kernel,
        name="place",
        out_shape=(jax.ShapeDtypeStruct((8, ROWS, 2 * COLS), bf16), jax.ShapeDtypeStruct((DEPTH, COLS), f32)),
        in_specs=[pl.BlockSpec(memory_space=pltpu.VMEM)] * 2,
        out_specs=(pl.BlockSpec(memory_space=pl.ANY),) * 2,
        scratch_shapes=[dma((2,))],
        compiler_params=pltpu.CompilerParams(vmem_limit_bytes=56 << 20),
    )(pltpu.with_memory_space_constraint(act, pltpu.VMEM), pltpu.with_memory_space_constraint(grad, pltpu.VMEM))
    return act.reshape(1, 8 * ROWS, 2 * COLS), grad


def solution(mesh):
    return jax.shard_map(
        local,
        mesh=mesh,
        in_specs=(P("ja", "ia", "ka"), P("ka", ("ia", "ja")), P("ja", None, ("ia", "ka"))),
        out_specs=(P("ja", None, ("ia", "ka")), P("ka", ("ia", "ja"))),
        check_vma=False,
    )
```

```python
import jax
import jax.numpy as jnp
from jax import lax
from jax.experimental import pallas as pl
from jax.experimental.pallas import tpu as pltpu
from jax.sharding import PartitionSpec as P

MESH = pl.DeviceIdType.MESH
ROWS, DEPTH, COLS = 48, 2048, 384
SPLIT = 256
DIRECT = 12
PAIRS = ((1, 7), (0, 2), (3, 5), (6, 4))
ORDER = (
    (0, 0), (0, 1), (1, 0), (3, 0), (1, 1), (3, 1), (2, 0), (0, 2),
    (0, 3), (2, 1), (1, 2), (3, 2), (2, 2), (1, 3), (3, 3), (2, 3),
)
CHUNKS = len(ORDER)
SLOT = {(dx, dz): (n, i) for n, (dx, p) in enumerate(ORDER) for i, dz in enumerate(PAIRS[p])}
OFF_X = tuple(dx for dx, _ in ORDER)
OFF_Z = tuple(PAIRS[p] for _, p in ORDER)
SCHEDULE = (
    ((("early_out", 0), ("early_x", 1), ("early_x", 3), ("early_out", 1), ("early_out", 3), ("z", 1),
      ("z", 7), ("x_out", 1), ("x_out", 7), ("early_z", 0, 1), ("early_z", 0, 7), ("x", 1, 0),
      ("x", 3, 0), ("sibling", 0, 1), ("sibling", 0, 7), ("sibling", 1, 0), ("sibling", 3, 0), ("early_x", 2),
      ("early_out", 2), ("early_z", 1, 1), ("early_z", 1, 7), ("early_z", 3, 1), ("early_z", 3, 7)), 0, 0, 0),
    ((("near",), ("z", 2), ("z", 6), ("x", 1, 1), ("x", 3, 1), ("x_out", 2),
      ("x_out", 6), ("sibling", 1, 1), ("sibling", 3, 1), ("early_z", 0, 2), ("early_z", 0, 6), ("sibling", 0, 2),
      ("sibling", 0, 6), ("combine", 0), ("early_z", 2, 1), ("early_z", 2, 7), ("early_z", 1, 2), ("early_z", 1, 6),
      ("early_z", 3, 2), ("early_z", 3, 6)), 0, 1, 0),
    ((("x", 1, 7), ("x", 3, 7), ("sibling", 1, 7), ("sibling", 3, 7)), 0, 2, 0),
    ((("x", 2, 0), ("sibling", 2, 0)), 0, 3, 0),
    ((("x", 2, 1), ("sibling", 2, 1), ("combine", 1)), 1, -1, 0),
    ((("combine", 2), ("combine", 3), ("x", 1, 2), ("x", 3, 2), ("sibling", 1, 2), ("sibling", 3, 2)), 2, -1, 0),
    ((("relay", 0), ("z", 3), ("z", 5), ("x_out", 3), ("x_out", 5), ("early_z", 0, 3),
      ("early_z", 0, 5), ("sibling", 0, 3), ("sibling", 0, 5)), 2, 4, 0),
    ((("early_z", 1, 3), ("early_z", 1, 5), ("early_z", 2, 2), ("early_z", 2, 6)), 2, 5, 0),
    ((("x", 1, 6), ("x", 3, 6), ("early_z", 3, 3), ("early_z", 3, 5), ("sibling", 1, 6), ("sibling", 3, 6),
      ("relay", 1)), 4, -1, 1),
    ((("x", 2, 7), ("sibling", 2, 7), ("combine", 4), ("z", 4), ("x_out", 4), ("cot_far",),
      ("early_z", 0, 4), ("sibling", 0, 4), ("early_z", 1, 4), ("combine", 5), ("x", 2, 2), ("sibling", 2, 2),
      ("early_z", 2, 3), ("early_z", 2, 5)), 4, 6, 1),
    ((("early_z", 3, 4), ("relay", 2)), 4, 7, 1),
    ((("relay", 3),), 4, 8, 1),
    ((), 4, 9, 1),
    ((("x", 1, 3), ("x", 3, 3), ("sibling", 1, 3), ("sibling", 3, 3), ("combine", 6)), 6, -1, 1),
    ((("combine", 7),), 6, -1, 2),
    ((("combine", 8),), 6, -1, 3),
    ((("x", 1, 5), ("x", 3, 5), ("sibling", 1, 5), ("sibling", 3, 5), ("combine", 9), ("early_z", 2, 4)), 7, -1, 3),
    ((("x", 2, 6), ("sibling", 2, 6)), 7, -1, 4),
    ((("relay", 4), ("relay", 5)), 7, 10, 4),
    ((), 7, 11, 4),
    ((("relay", 6),), 8, -1, 4),
    ((("x", 1, 4), ("x", 3, 4), ("sibling", 1, 4), ("sibling", 3, 4)), 10, -1, 5),
    ((("x", 2, 3), ("sibling", 2, 3), ("combine", 10)), 10, -1, 6),
    ((("x", 2, 5), ("sibling", 2, 5), ("combine", 11), ("relay", 7)), 10, -1, 7),
    ((), 10, 12, 7),
    ((("x", 2, 4), ("sibling", 2, 4), ("relay", 8), ("relay", 9)), 10, 13, 7),
    ((), 10, 14, 7),
    ((), 10, 15, 7),
    ((("combine", 12),), 12, -1, 8),
    ((("combine", 13), ("combine", 14)), 12, -1, 9),
    ((("combine", 15),), 12, -1, 10),
    ((("relay", 10),), 13, -1, 10),
    ((("relay", 11),), 16, -1, 16),
)


def pick(index, table):
    if isinstance(index, int):
        return table[index]
    out = jnp.int32(table[0])
    for j, entry in enumerate(table[1:], 1):
        out = jnp.where(index == j, jnp.int32(entry), out)
    return out


def mod(value, n):
    return lax.rem(value + 16 * n, n)


def kernel(tok_ref, w_ref, cot_ref, act_ref, grad_ref, xs, ws, cots, hop, mine, pf, pb, terms, slopes, acts,
           load_sem, z_send, z_recv, x_send, x_recv, ez_send, ez_recv, ex_send, ex_recv, sib_send, sib_recv, rs_send, rs_recv, ag_send, ag_recv,
           hop_send, hop_recv, mine_send, mine_recv, act_send, act_recv):
    ia, ja, y = lax.axis_index("ia"), lax.axis_index("ja"), lax.axis_index("ka")
    x, z_lo, z_hi, c = ia // 2, lax.rem(ia, 2), ja // 2, lax.rem(ja, 2)
    z = z_hi * 2 + z_lo

    def device(dx=0, dz=0, dy=0):
        tz = mod(z + dz, 8)
        return (mod(x + dx, 4) * 2 + lax.rem(tz, 2), (tz // 2) * 2 + c, mod(y + dy, 4))

    sibling = (ia, z_hi * 2 + 1 - c, y)

    def remote(src, dst, send, recv, to):
        return pltpu.make_async_remote_copy(
            src_ref=src, dst_ref=dst, send_sem=send, recv_sem=recv, device_id=to, device_id_type=MESH)

    loads = [
        pltpu.make_async_copy(tok_ref, xs.at[SLOT[0, 0][0], SLOT[0, 0][1], 0], load_sem.at[0]),
        pltpu.make_async_copy(cot_ref, cots, load_sem.at[1]),
        pltpu.make_async_copy(w_ref, ws, load_sem.at[2]),
    ]
    for load in loads:
        load.start()

    barrier = pltpu.get_barrier_semaphore()
    for to in [device(dx=1), device(dx=-1), device(dz=1), device(dz=-1)] + [device(dy=r) for r in (1, 2, 3)] + [
            (ia, mod(ja + d, 8), y) for d in range(1, 8)]:
        pl.semaphore_signal(barrier, inc=1, device_id=to, device_id_type=MESH)
    at_home = y == z_hi
    for owner in range(4):
        for core in range(2):
            @pl.when(jnp.logical_not(at_home & (owner == y) & (core == c)))
            def _():
                pl.semaphore_signal(barrier, inc=1, device_id=(ia, y * 2 + core, owner), device_id_type=MESH)
    pl.semaphore_wait(barrier, 14 + 8 - jnp.where(at_home, 1, 0))

    def block(dx, dz, core=0):
        n, i = SLOT[dx, dz]
        return xs.at[n, i, core]

    def early(ref, h=None):
        return ref.at[:, pl.ds(0, SPLIT)] if h is None else ref.at[:, pl.ds(h * (SPLIT // 2), SPLIT // 2)]

    def late(ref, h=None):
        size = (DEPTH - SPLIT) // 2
        return ref.at[:, pl.ds(SPLIT, 2 * size)] if h is None else ref.at[:, pl.ds(SPLIT + h * size, size)]

    def along_z(part, dx, dz, way, sends, recvs):
        to, h = (dz + way) % 8, (None if (dz + way) % 8 != 4 else (0 if way == 1 else 1))
        at = to if h is None else 4 * h
        return remote(part(block(dx, dz), h), part(block(dx, to), h), sends.at[dx, at], recvs.at[dx, at], device(dz=way))

    def along_x(part, dz, dx, way, sends, recvs):
        to, h = (dx + way) % 4, (None if (dx + way) % 4 != 2 else (0 if way == 1 else 1))
        at = to if h is None else 2 * h
        return remote(part(block(dx, dz), h), part(block(to, dz), h), sends.at[at, dz], recvs.at[at, dz], device(dx=way))

    def z_late(dz, way):
        return along_z(late, 0, dz, way, z_send, z_recv)

    def x_late(dz, dx, way):
        return along_x(late, dz, dx, way, x_send, x_recv)

    def x_early(dx, way):
        return along_x(early, 0, dx, way, ex_send, ex_recv)

    def z_early(dx, dz, way):
        return along_z(early, dx, dz, way, ez_send, ez_recv)

    def sib_copy(n, i):
        return remote(xs.at[n, i, 0], xs.at[n, i, 1], sib_send.at[n, i], sib_recv.at[n, i], sibling)

    def to_sibling(dx, dz):
        sib_copy(*SLOT[dx, dz]).start()

    def ring_step(copy, at, size):
        if at == size // 2:
            copy(at - 1, 1).wait_recv()
            copy(at + 1, -1).wait_recv()
        else:
            way = 1 if at < size // 2 else -1
            copy((at - way) % size, way).wait_recv()
            copy(at, way).start()

    def z_arrive(dz):
        ring_step(z_late, dz, 8)

    def x_out(*dzs):
        for dz in dzs:
            x_late(dz, 0, 1).start()
            x_late(dz, 0, -1).start()

    def x_arrive(dx, dz):
        ring_step(lambda at, way: x_late(dz, at, way), dx, 4)

    def early_x(dx):
        ring_step(x_early, dx, 4)

    def early_out(dx):
        z_early(dx, 0, 1).start()
        z_early(dx, 0, -1).start()

    def early_z(dx, dz):
        ring_step(lambda at, way: z_early(dx, at, way), dz, 8)

    def to_mine(dz, other, b):
        tz, tc = mod(z_hi + dz, 4), (1 - c if other else c)
        src = hop.at[mod(y - tz, 4), b, :, pl.ds(pl.multiple_of(tc * COLS, COLS), COLS)]
        d = dz * 2 + other
        if d == 0:
            return pltpu.make_async_copy(src, mine.at[0, b], mine_recv.at[0, b])
        return remote(src, mine.at[d, b], mine_send.at[d, b], mine_recv.at[d, b], (ia, tz * 2 + tc, y))

    def to_hop(r, b):
        at = mod(y + r - z_hi * 2 - b - c, 4) * 2 + b
        if r == 0:
            return pltpu.make_async_copy(cots.at[at], hop.at[0, b], hop_recv.at[0, b])
        return remote(cots.at[at], hop.at[r, b], hop_send.at[r, b], hop_recv.at[r, b], device(dy=r))

    def cot_near():
        for r in range(4):
            for b in range(2):
                to_hop(r, b).wait_recv() if r else to_hop(r, b).wait()
        for dz in (0, 1, 3):
            for other in (0, 1):
                for b in range(2):
                    to_mine(dz, other, b).start()

    def cot_far():
        for other in (0, 1):
            for b in range(2):
                to_mine(2, other, b).start()

    loads[0].wait()
    for way in (1, -1):
        z_late(0, way).start()
    for way in (1, -1):
        x_early(0, way).start()
    x_out(0)
    to_sibling(0, 0)
    loads[1].wait()
    for r in range(4):
        for b in range(2):
            to_hop(r, b).start()
    grad_ref[...] = jnp.zeros_like(grad_ref)
    loads[2].wait()

    def place(n, r):
        first = pick(n, [pair[0] for pair in OFF_Z])
        v = mod(y + r - x + pick(n, OFF_X) - z + first, 4)
        i = v // 2
        return i, lax.rem(v + c, 2)

    def way_of(n):
        return 1 + 2 * (n % 2)

    def rs_far(n):
        i, k = place(n, 2)
        return remote(pb.at[n, i, k], terms.at[n, 2], rs_send.at[n, 2], rs_recv.at[n, 2], device(dy=way_of(n)))

    def rs_sum(n):
        i, k = place(n, way_of(n))
        return remote(pb.at[n, i, k], terms.at[n, 0], rs_send.at[n, 0], rs_recv.at[n, 0], device(dy=way_of(n)))

    def rs_near(n):
        i, k = place(n, 4 - way_of(n))
        return remote(pb.at[n, i, k], terms.at[n, 1], rs_send.at[n, 1], rs_recv.at[n, 1], device(dy=4 - way_of(n)))

    def combine(n):
        rs_far(n).wait_recv()
        i, k = place(n, way_of(n))
        pb[n, i, k] = (pf[n, i, k] + terms[n, 2].astype(jnp.float32)).astype(jnp.bfloat16)
        rs_sum(n).start()

    def ag_copy(n, way):
        i, k = place(n, 0)
        return remote(slopes.at[n, i, k], slopes.at[n, i, k], ag_send.at[n, way - 1], ag_recv.at[n, way - 1],
                      device(dy=way))

    def ag_second(n):
        way = way_of(n)
        i, k = place(n, 4 - way)
        return remote(slopes.at[n, i, k], slopes.at[n, i, k], ag_send.at[n, 1], ag_recv.at[n, 1], device(dy=way))

    def ag_direct(n):
        i, k = place(n, 0)
        return remote(slopes.at[n, i, k], slopes.at[n, i, k], ag_send.at[n, 1], ag_recv.at[n, 1], device(dy=2))

    def relay(n):
        ag_copy(n, 1 + 2 * (n % 2)).wait_recv()
        ag_second(n).start()

    def source(n):
        i, k = place(n, 0)
        dz = jnp.where(i == 0, pick(n, [pair[0] for pair in OFF_Z]), pick(n, [pair[1] for pair in OFF_Z]))
        return mod(x - pick(n, OFF_X), 4), mod(z - dz, 8), lax.rem(c + k, 2)

    def act_copies(n):
        sx, sz, sc = source(n)
        at = sx * 2 + lax.rem(sz, 2)
        dst = act_ref.at[at, :, pl.ds(pl.multiple_of(c * COLS, COLS), COLS)]
        here = at_home & (sz // 2 == z_hi) & (sc == c)
        to = (ia, (sz // 2) * 2 + sc, z_hi)
        return (here, pltpu.make_async_copy(acts.at[n], dst, act_recv.at[at, c]),
                remote(acts.at[n], dst, act_send.at[n], act_recv.at[at, c], to))

    def forward(n):
        for i in range(2):
            sib_copy(n, i).wait_recv()
        out = jnp.dot(xs[n].reshape(4 * ROWS, DEPTH), ws[...], preferred_element_type=jnp.float32)
        pf[n] = out.reshape(2, 2, ROWS, COLS)
        pb[n] = out.astype(jnp.bfloat16).reshape(2, 2, ROWS, COLS)
        rs_far(n).start()
        rs_near(n).start()

    def middle(n):
        rs_near(n).wait_recv()
        rs_sum(n).wait_recv()
        i, k = place(n, 0)
        _, sz, sc = source(n)
        pre = pf[n, i, k] + terms[n, 0].astype(jnp.float32) + terms[n, 1].astype(jnp.float32)
        d, b = mod(z_hi - sz // 2, 4) * 2 + lax.rem(sc + c, 2), lax.rem(sz, 2)
        pltpu.make_async_copy(mine.at[d, b], mine.at[d, b], mine_recv.at[d, b]).wait()
        cot = mine[d, b].astype(jnp.float32)
        root = 0.7978845608028654
        square = pre * pre
        t = jnp.tanh(root * pre * (1.0 + 0.044715 * square))
        slope = 0.5 * (1.0 + t) + 0.5 * pre * (1.0 - t * t) * (root * (1.0 + 3 * 0.044715 * square))
        slopes[n, i, k] = (cot * slope).astype(jnp.bfloat16)
        for r in (1, 3):
            ag_copy(n, r).start()
        if n >= DIRECT:
            ag_direct(n).start()
        acts[n] = (0.5 * pre * (1.0 + t)).astype(jnp.bfloat16)
        here, local_copy, remote_copy = act_copies(n)
        pl.when(here)(local_copy.start)
        pl.when(jnp.logical_not(here))(remote_copy.start)

    def backward(n):
        ag_copy(n, 3 - 2 * (n % 2)).wait_recv()
        ag_second(n).wait_recv()
        if n >= DIRECT:
            ag_copy(n, 1 + 2 * (n % 2)).wait_recv()
        s = slopes[n].reshape(4 * ROWS, COLS)
        for b in range(4):
            cols = pl.ds(b * 512, 512)
            grad_ref[cols, :] += lax.dot_general(
                xs[n, :, :, :, cols].reshape(4 * ROWS, 512), s, (((0,), (0,)), ((), ())),
                preferred_element_type=jnp.float32)

    actions = {
        "z": z_arrive, "x_out": x_out, "x": x_arrive, "early_x": early_x, "early_out": early_out, "early_z": early_z,
        "sibling": to_sibling,
        "near": cot_near, "cot_far": cot_far, "relay": relay, "combine": combine,
    }
    mids, grads = [0], [0]
    for _, mid, _, grad in SCHEDULE:
        mids.append(mid)
        grads.append(grad)

    def drain_tokens():
        for dz in (0, 1, 2, 3, 7, 6, 5):
            for way in ((1, -1) if dz == 0 else (1,) if dz < 4 else (-1,)):
                z_late(dz, way).wait_send()
                for dx in range(4):
                    z_early(dx, dz, way).wait_send()
        for dx, way in ((0, 1), (0, -1), (1, 1), (3, -1)):
            x_early(dx, way).wait_send()
            for dz in range(8):
                x_late(dz, dx, way).wait_send()
        for r in range(1, 4):
            for b in range(2):
                to_hop(r, b).wait_send()
        for d in range(2, 16):
            to_mine(d // 4, d // 2 % 2, d % 2).wait_send()

    def drain_chunk(n):
        for copy in (sib_copy(n, 0), sib_copy(n, 1)):
            copy.wait_send()
        for j in range(3):
            remote(pb.at[n, 0, 0], terms.at[n, j], rs_send.at[n, j], rs_recv.at[n, j], sibling).wait_send()
            remote(slopes.at[n, 0, 0], slopes.at[n, 0, 0], ag_send.at[n, j], ag_recv.at[n, j], sibling).wait_send()

    def drain_act(n):
        here, _, remote_copy = act_copies(n)
        pl.when(jnp.logical_not(here))(remote_copy.wait_send)

    for t, (events, _, chunk, _) in enumerate(SCHEDULE):
        for name, *args in events:
            actions[name](*args)
        for n in range(mids[t], mids[t + 1]):
            middle(n)
        if chunk >= 0:
            forward(chunk)
        for n in range(grads[t], grads[t + 1]):
            backward(n)
            if n == 10:
                drain_tokens()
            drain_chunk(n)
            if n >= 2:
                drain_act(n - 2)

    for n in (CHUNKS - 2, CHUNKS - 1):
        drain_act(n)
    for at in range(8):
        for core in range(2):
            dst = act_ref.at[at, :, pl.ds(core * COLS, COLS)]
            pltpu.make_async_copy(acts.at[0], dst, act_recv.at[at, core]).wait()


def place_kernel(act_in, grad_in, act_out, grad_out, sem):
    copies = [pltpu.make_async_copy(act_in, act_out, sem.at[0]), pltpu.make_async_copy(grad_in, grad_out, sem.at[1])]
    for copy in copies:
        copy.start()
    for copy in copies:
        copy.wait()


def local(tokens, weight_up, cotangent):
    dma = pltpu.SemaphoreType.DMA
    bf16, f32 = jnp.bfloat16, jnp.float32
    act, grad = pl.pallas_call(
        kernel,
        name="mlp_up",
        out_shape=(pltpu.VMEM((8, ROWS, 2 * COLS), bf16), pltpu.VMEM((DEPTH, COLS), f32)),
        in_specs=[pl.BlockSpec(memory_space=pl.ANY)] * 3,
        out_specs=(pl.BlockSpec(memory_space=pltpu.VMEM),) * 2,
        scratch_shapes=[
            pltpu.VMEM((CHUNKS, 2, 2, ROWS, DEPTH), bf16),
            pltpu.VMEM((DEPTH, COLS), bf16),
            pltpu.VMEM((8, ROWS, 2 * COLS), bf16),
            pltpu.VMEM((4, 2, ROWS, 2 * COLS), bf16),
            pltpu.VMEM((8, 2, ROWS, COLS), bf16),
            pltpu.VMEM((CHUNKS, 2, 2, ROWS, COLS), f32),
            pltpu.VMEM((CHUNKS, 2, 2, ROWS, COLS), bf16),
            pltpu.VMEM((CHUNKS, 3, ROWS, COLS), bf16),
            pltpu.VMEM((CHUNKS, 2, 2, ROWS, COLS), bf16),
            pltpu.VMEM((CHUNKS, ROWS, COLS), bf16),
            dma((3,)),
            dma((1, 8)), dma((1, 8)),
            dma((4, 8)), dma((4, 8)),
            dma((4, 8)), dma((4, 8)),
            dma((4, 1)), dma((4, 1)),
            dma((CHUNKS, 2)), dma((CHUNKS, 2)),
            dma((CHUNKS, 3)), dma((CHUNKS, 3)),
            dma((CHUNKS, 3)), dma((CHUNKS, 3)),
            dma((4, 2)), dma((4, 2)),
            dma((8, 2)), dma((8, 2)),
            dma((CHUNKS,)), dma((8, 2)),
        ],
        compiler_params=pltpu.CompilerParams(
            collective_id=0, has_side_effects=True, vmem_limit_bytes=56 << 20),
    )(tokens.reshape(ROWS, DEPTH), weight_up, cotangent.reshape(8, ROWS, 2 * COLS))
    act, grad = pl.pallas_call(
        place_kernel,
        name="place",
        out_shape=(jax.ShapeDtypeStruct((8, ROWS, 2 * COLS), bf16), jax.ShapeDtypeStruct((DEPTH, COLS), f32)),
        in_specs=[pl.BlockSpec(memory_space=pltpu.VMEM)] * 2,
        out_specs=(pl.BlockSpec(memory_space=pl.ANY),) * 2,
        scratch_shapes=[dma((2,))],
        compiler_params=pltpu.CompilerParams(vmem_limit_bytes=56 << 20),
    )(pltpu.with_memory_space_constraint(act, pltpu.VMEM), pltpu.with_memory_space_constraint(grad, pltpu.VMEM))
    return act.reshape(1, 8 * ROWS, 2 * COLS), grad


def solution(mesh):
    return jax.shard_map(
        local,
        mesh=mesh,
        in_specs=(P("ja", "ia", "ka"), P("ka", ("ia", "ja")), P("ja", None, ("ia", "ka"))),
        out_specs=(P("ja", None, ("ia", "ka")), P("ka", ("ia", "ja"))),
        check_vma=False,
    )
```
